32 devices in a mesh: ctx: 8 (over z, y), head: 4 (over x, core).
Axes of the slice: x: 2, y: 2, z: 4, core: 2. Of those that a mesh axis runs over, the one named last changes fastest.
Arguments:
- queries: bfloat16 [2048, 4096], P('ctx', 'head'), may hold values from -8 to 8
- keys: bfloat16 [2048, 1024], P('ctx', 'head'), may hold values from -6 to 6
- values: bfloat16 [2048, 1024], P('ctx', 'head'), may hold values from -6 to 6
- segment_ids: int32 [2048], P('ctx'), may hold values from 0 to 31, never falling along the last dimension, each value on 1 to 256 neighbouring positions
- out_weight: bfloat16 [4096, 4096], P('head'), may hold values from -0.125 to 0.125
Outputs:
- mixed: bfloat16 [2048, 4096], P('ctx', 'head')
The draws below stay inside these ranges and needn't reach their ends.
Inputs may be any that keep to these rules, and one draw needn't show every extreme that they name: `segment_ids`: documents are contiguous runs of tokens; none is longer than 256 tokens and one is exactly that long.
All inputs are finite; a program needn't handle non-finite values.
Results may differ from the reference program's by a relative error of at most 0.015.
Values may be sent and summed in bfloat16 or wider, within the bound.
No kernel may reach another device: no remote copies, remote signals or barrier semaphores. Data moves between devices by JAX's collectives and lax.ppermute only.
A program may use at most 64 MiB of HBM per device.

```python
import math
import jax
import jax.numpy as jnp
import numpy as np
from jax import lax

D = 4096
HEADS = 32
KV_HEADS = 8
HEAD_DIM = 128
SEGS = 32
SEQ = 2048
DOC_MAX = 256


def draw_queries(key, part):
    inner = jax.random.fold_in(key, 3)
    result = jnp.clip(2.0 * jax.random.normal(inner, (SEQ, HEADS * HEAD_DIM), jnp.float32), -8.0, 8.0)
    return result.astype(jnp.bfloat16)


def draw_keys(key, part):
    inner = jax.random.fold_in(key, 5)
    result = jnp.clip(jax.random.normal(inner, (SEQ, KV_HEADS, HEAD_DIM), jnp.float32), -6.0, 6.0)
    return result.reshape(SEQ, KV_HEADS * HEAD_DIM).astype(jnp.bfloat16)


def with_spikes(values, own_key, source, target, blocks, factor):
    owner, partner = [(jnp.arange(values.shape[axis_at]) // (values.shape[axis_at] // blocks)).reshape([-1 if axis == axis_at else 1 for axis in range(values.ndim)]) for axis_at in (source, target)]
    chosen = jax.random.permutation(own_key, blocks)[partner]
    strong = (owner == chosen) | (owner == (partner + blocks // 2) % blocks)
    return jnp.where(strong, factor * values, values)


def levels(rng, extent, cuts, low, largest):
    def one(axis_at, shards_of):
        draws = jax.random.uniform(jax.random.fold_in(jax.random.fold_in(rng, 6), axis_at), (shards_of,), jnp.float32, low / len(cuts), largest / len(cuts))
        return jnp.repeat(jnp.exp(draws), extent[axis_at] // shards_of).reshape((-1,) + (1,) * (len(extent) - axis_at - 1))

    loudness = one(*cuts[0])
    for cut in cuts[1:]:
        loudness = loudness * one(*cut)
    return loudness


def split_up(amount, total, most, lean):
    weights = [(1 << 20) // math.isqrt(grade ** lean) + 1 for grade in range(2, amount + 1)]
    rest, counts = total - most - (amount - 1), [1] * (amount - 1)
    while rest > 0:
        candidates = [i for i in range(amount - 1) if counts[i] < most]
        pool, budget = sum([weights[i] for i in candidates]), rest
        for i in candidates:
            extra = min(most - counts[i], max(1, budget * weights[i] // pool), rest)
            counts[i] = counts[i] + extra
            rest = rest - extra
    return np.array([most] + counts)


def ragged_sizes(rng, count, total, most, lean):
    if count == 2:
        one = jax.random.randint(rng, (), max(1, total - most), min(most, total - 1) + 1)
        return jnp.stack([one, total - one])
    sizes = jnp.asarray(split_up(count, total, most, lean), jnp.int32)
    twos = (count - 1) // 2
    source_of, sink = sizes[1:1 + 2 * twos:2], sizes[2:2 + 2 * twos:2]
    margin = jnp.minimum(source_of - 1, most - sink)
    moved = jax.random.randint(jax.random.fold_in(rng, 1), (twos,), 0, 1 << 20) % (margin + 1)
    sizes = sizes.at[1:1 + 2 * twos:2].set(source_of - moved).at[2:2 + 2 * twos:2].set(sink + moved)
    return sizes[jax.random.permutation(jax.random.fold_in(rng, 2), count)]


def normal_values(key, dims, spread, most, shards=(), held_as=jnp.bfloat16):
    entries = jax.random.normal(key, dims, jnp.float32) * spread
    if len(shards) > 0:
        entries = levels(key, dims, shards, -0.22, 0.18) * entries
    return jnp.clip(entries, min=-most, max=most).astype(held_as)


def noise_with(stream_key, extent, spread, bound, cuts, heavy, kind=jnp.bfloat16):
    drawn = spread * jax.random.normal(stream_key, extent, jnp.float32)
    if cuts:
        drawn = drawn * levels(stream_key, extent, cuts, -0.22, 0.18)
    return jnp.clip(with_spikes(drawn, jax.random.fold_in(stream_key, 3), *heavy), -bound, bound).astype(kind)


def setup_inputs(seed: int = 0) -> dict:
    key_list = jax.random.split(jax.random.key(seed), 6)
    return {
        "queries": draw_queries(jax.random.fold_in(key_list[5], 71), 0),
        "keys": draw_keys(jax.random.fold_in(key_list[5], 71), 0),
        "values": normal_values(key_list[2], (SEQ, KV_HEADS * HEAD_DIM), 1.0, 6.0, ((0, 8), (1, 4))),
        "segment_ids": jnp.searchsorted(jnp.cumsum(ragged_sizes(key_list[3], SEGS, SEQ, DOC_MAX, 1)), jnp.arange(SEQ), side="right").astype(jnp.int32),
        "out_weight": noise_with(key_list[4], (D, D), D ** -0.5, 0.125, ((0, 4),), (0, 1, 4, 2.0)),
    }


def reference(queries, keys, values, segment_ids, out_weight):
    block = math.gcd(SEQ, 256)
    width = min(SEQ, DOC_MAX + block)
    groups = HEADS // KV_HEADS
    scale = 1.0 / math.sqrt(HEAD_DIM)

    def one_block(index):
        start = (index * block).astype(jnp.int32)
        kstart = jnp.clip(start + block - width, 0, SEQ - width).astype(jnp.int32)
        query = lax.dynamic_slice_in_dim(queries, start, block, 0).astype(jnp.float32)
        query = query.reshape(block, KV_HEADS, groups, HEAD_DIM)
        keyset = lax.dynamic_slice_in_dim(keys, kstart, width, 0).astype(jnp.float32)
        keyset = keyset.reshape(width, KV_HEADS, HEAD_DIM)
        valset = lax.dynamic_slice_in_dim(values, kstart, width, 0).astype(jnp.float32)
        valset = valset.reshape(width, KV_HEADS, HEAD_DIM)
        qpos = start + jnp.arange(block, dtype=jnp.int32)
        kpos = kstart + jnp.arange(width, dtype=jnp.int32)
        qseg = lax.dynamic_slice_in_dim(segment_ids, start, block, 0)
        kseg = lax.dynamic_slice_in_dim(segment_ids, kstart, width, 0)
        visible = (kpos[None, :] <= qpos[:, None]) & (kseg[None, :] == qseg[:, None])
        scores = jnp.einsum('qgrd,kgd->grqk', query, keyset) * scale
        top = lax.optimization_barrier(jnp.max(jnp.where(visible, scores, -1e+30), axis=-1))
        weights = jnp.where(visible, jnp.exp(scores - top[..., None]), 0.0)
        total = lax.optimization_barrier(jnp.sum(weights, axis=-1))
        rounded = lax.optimization_barrier(weights.astype(jnp.bfloat16)).astype(jnp.float32)
        summed = jnp.einsum('grqk,kgd->qgrd', rounded, valset)
        attended = summed / jnp.transpose(total, (2, 0, 1))[..., None]
        return attended.reshape(block, HEADS * HEAD_DIM).astype(jnp.bfloat16)
    blocks = lax.map(one_block, jnp.arange(SEQ // block, dtype=jnp.int32))
    attended = blocks.reshape(SEQ, HEADS * HEAD_DIM)
    return jnp.dot(attended, out_weight, preferred_element_type=jnp.float32).astype(jnp.bfloat16)
```

```python
import math

import jax
import jax.numpy as jnp
from jax import lax
from jax.experimental import pallas as pl
from jax.experimental.pallas import tpu as pltpu
from jax.sharding import PartitionSpec as P

HEAD_DIM = 128
CORES = 2
HALVES = 2
DOC_ROWS = 16
LOG2_SCALE = math.log2(math.e) / math.sqrt(HEAD_DIM)
HIDDEN = -1e30
NT = (((1,), (1,)), ((), ()))
VMEM = pl.BlockSpec(memory_space=pltpu.VMEM)
ANY = pl.BlockSpec(memory_space=pl.ANY)
HBM = pl.BlockSpec(memory_space=pltpu.HBM)


def near(x):
    return pltpu.with_memory_space_constraint(x, pltpu.VMEM)


def far(x):
    return pltpu.with_memory_space_constraint(x, pltpu.HBM)


def call(kernel, out_shape, in_specs, args, flops, bytes_accessed, vmem_mib=16, scratch=()):
    return pl.pallas_call(
        kernel,
        out_shape=out_shape,
        in_specs=in_specs,
        out_specs=jax.tree.map(lambda _: VMEM, out_shape),
        scratch_shapes=scratch,
        compiler_params=pltpu.CompilerParams(vmem_limit_bytes=vmem_mib * 2**20),
        cost_estimate=pl.CostEstimate(
            flops=flops, bytes_accessed=bytes_accessed, transcendentals=0
        ),
    )(*args)


def pack_kernel(k_ref, v_ref, doc_ref, out_ref, held, sem):
    tokens, width = k_ref.shape
    copies = [
        pltpu.make_async_copy(k_ref, out_ref.at[:tokens], sem.at[0]),
        pltpu.make_async_copy(v_ref, out_ref.at[tokens : 2 * tokens], sem.at[1]),
        pltpu.make_async_copy(doc_ref, held, sem.at[2]),
    ]
    for copy in copies:
        copy.start()
    copies[2].wait()
    rows = [
        (held[:, i * width : (i + 1) * width] + 1).astype(jnp.float32)
        for i in range(tokens // width)
    ]
    rows.append(jnp.zeros((DOC_ROWS - len(rows), width), jnp.float32))
    out_ref[2 * tokens :, :] = jnp.concatenate(rows, axis=0).astype(jnp.bfloat16)
    copies[0].wait()
    copies[1].wait()


def doc_column(docs):
    count = docs.shape[1]
    return jnp.transpose(jnp.broadcast_to(docs, (count, count)))[:, :1]


def stacked(q_ref, r0, rows, first, repeats):
    heads = [
        q_ref[r0 : r0 + rows, h * HEAD_DIM : (h + 1) * HEAD_DIM]
        for h in range(first, first + repeats)
    ]
    return jnp.concatenate(heads, axis=0)


def with_ones(v):
    return jnp.concatenate([v, jnp.ones_like(v)], axis=1)


def hide(scores, bias):
    rows, count = bias.shape
    shape = (scores.shape[0] // rows, rows, count)
    return (scores.reshape(shape) + bias[None]).reshape(scores.shape)


def weights_of(scores, top):
    return jnp.exp2((scores - top) * LOG2_SCALE).astype(jnp.bfloat16)


def own_kernel(
    chips, q_hbm, k_hbm, v_hbm, doc_hbm, w_ref,
    acc_ref, top_ref, total_ref, q_ref, doc_ref, held_ref, k_ref, v_ref, in_sem, sem,
):
    inputs = [
        pltpu.make_async_copy(source, target, in_sem.at[i])
        for i, (source, target) in enumerate(
            ((doc_hbm, doc_ref), (q_hbm, q_ref), (k_hbm, k_ref), (v_hbm, v_ref))
        )
    ]
    for copy in inputs:
        copy.start()
    me = lax.axis_index("head")
    chip, core = me // CORES, me % CORES
    block = w_ref.shape[1] // (chips * CORES)
    copies = []
    for d in range(chips):
        for which in range(CORES):
            target = lax.rem(chip + d, chips) * CORES + lax.rem(core + which, CORES)
            start = pl.multiple_of(target * block, block)
            copy = pltpu.make_async_copy(
                w_ref.at[:, pl.ds(start, block)], held_ref.at[d, which], sem.at[d, which]
            )
            copy.start()
            copies.append(copy)
    for copy in inputs:
        copy.wait()

    tokens, width = q_ref.shape
    groups = k_ref.shape[1] // HEAD_DIM
    repeats = width // HEAD_DIM // groups
    rows = tokens // HALVES
    docs = doc_ref[...].astype(jnp.float32)
    column = doc_column(docs)
    for half in range(HALVES):
        r0, count = half * rows, (half + 1) * rows
        at = r0 + lax.broadcasted_iota(jnp.int32, (rows, count), 0)
        key = lax.broadcasted_iota(jnp.int32, (rows, count), 1)
        visible = (key <= at) & (docs[:, :count] == column[r0 : r0 + rows])
        bias = jnp.where(visible, 0.0, HIDDEN)
        for g in range(groups):
            lanes = slice(g * HEAD_DIM, (g + 1) * HEAD_DIM)
            q = stacked(q_ref, r0, rows, g * repeats, repeats)
            scores = lax.dot_general(q, k_ref[:count, lanes], NT, preferred_element_type=jnp.float32)
            scores = hide(scores, bias)
            top = jnp.max(scores, axis=1, keepdims=True)
            v1 = with_ones(v_ref[:count, lanes])
            summed = jnp.dot(weights_of(scores, top), v1, preferred_element_type=jnp.float32)
            acc_ref[half, g] = summed[:, :HEAD_DIM]
            total_ref[half, g] = summed[:, HEAD_DIM:]
            top_ref[half, g] = jnp.broadcast_to(top, (q.shape[0], HEAD_DIM))
    for copy in copies:
        copy.wait()


def cross_kernel(q_ref, doc_ref, acc_ref, top_ref, total_ref, *rest):
    prev_refs, att_ref = rest[:-1], rest[-1]
    tokens, width = q_ref.shape
    groups = prev_refs[0].shape[1] // HEAD_DIM
    repeats = width // HEAD_DIM // groups
    rows = tokens // HALVES
    column = doc_column(doc_ref[...].astype(jnp.float32))
    key_docs = []
    for prev in prev_refs:
        wide = prev[2 * tokens : 2 * tokens + DOC_ROWS, :].astype(jnp.float32)
        parts = [wide[i : i + 1, :] for i in range(tokens // prev.shape[1])]
        key_docs.append(jnp.concatenate(parts, axis=1) - 1.0)
    for half in reversed(range(HALVES)):
        r0 = half * rows
        for g in range(groups):
            lanes = slice(g * HEAD_DIM, (g + 1) * HEAD_DIM)
            q = stacked(q_ref, r0, rows, g * repeats, repeats)
            acc, top, total = acc_ref[half, g], top_ref[half, g], total_ref[half, g]
            for i, prev in enumerate(prev_refs):
                first = r0 if i == len(prev_refs) - 1 else 0
                visible = key_docs[i][:, first:] == column[r0 : r0 + rows]
                bias = jnp.where(visible, 0.0, HIDDEN)
                scores = lax.dot_general(
                    q, prev[first:tokens, lanes], NT, preferred_element_type=jnp.float32
                )
                scores = hide(scores, bias)
                fresh = jnp.maximum(top, jnp.max(scores, axis=1, keepdims=True))
                factor = jnp.exp2((top - fresh) * LOG2_SCALE)
                v1 = with_ones(prev[tokens + first : 2 * tokens, lanes])
                summed = jnp.dot(
                    weights_of(scores, fresh[:, :1]), v1, preferred_element_type=jnp.float32
                )
                acc = acc * factor + summed[:, :HEAD_DIM]
                total = total * factor + summed[:, HEAD_DIM:]
                top = fresh
            result = (acc / total).astype(jnp.bfloat16)
            for r in range(repeats):
                h = g * repeats + r
                att_ref[r0 : r0 + rows, h * HEAD_DIM : (h + 1) * HEAD_DIM] = result[
                    r * rows : (r + 1) * rows
                ]


def project_kernel(d, c0, att_ref, held_ref, *rest):
    keep_ref, give_ref = rest[-2:]
    cols = keep_ref.shape[1]
    att = att_ref[...]
    for which, out in ((1, give_ref), (0, keep_ref)):
        out[...] = jnp.dot(
            att, held_ref[d, which, :, c0 : c0 + cols], preferred_element_type=jnp.float32
        ).astype(jnp.bfloat16)


def body(queries, keys, values, segment_ids, out_weight):
    tokens, width = queries.shape
    kv_width = keys.shape[1]
    groups = kv_width // HEAD_DIM
    place_count = lax.axis_size("ctx")
    devices = lax.axis_size("head")
    chips = devices // CORES
    rows, columns = out_weight.shape
    block = columns // devices
    span = max(place_count // 16, 2)
    bf16, f32 = jnp.bfloat16, jnp.float32
    dma = pltpu.SemaphoreType.DMA

    doc_row = segment_ids.reshape(1, tokens)
    packed = call(
        pack_kernel,
        pltpu.VMEM((2 * tokens + DOC_ROWS, kv_width), bf16),
        [HBM] * 3,
        (far(keys), far(values), far(doc_row)),
        0,
        8 * tokens * kv_width,
        scratch=[pltpu.VMEM((1, tokens), jnp.int32), dma((3,))],
    )
    prevs = [
        lax.ppermute(packed, "ctx", [(i, i + s) for i in range(place_count - s)])
        for s in range(1, span)
    ]

    attention_flops = 4 * tokens * tokens * width
    state = pltpu.VMEM((HALVES, groups, tokens // HALVES * (width // kv_width), HEAD_DIM), f32)
    acc, top, total, near_q, near_doc, held = call(
        lambda *refs: own_kernel(chips, *refs),
        [
            state,
            state,
            state,
            pltpu.VMEM((tokens, width), bf16),
            pltpu.VMEM((1, tokens), jnp.int32),
            pltpu.VMEM((chips, CORES, rows, block), bf16),
        ],
        [HBM] * 5,
        (far(queries), far(keys), far(values), far(doc_row), far(out_weight)),
        attention_flops,
        2 * rows * columns,
        scratch=[
            pltpu.VMEM((tokens, kv_width), bf16),
            pltpu.VMEM((tokens, kv_width), bf16),
            dma((4,)),
            dma((chips, CORES)),
        ],
    )

    att = call(
        cross_kernel,
        pltpu.VMEM((tokens, width), bf16),
        [VMEM] * (5 + len(prevs)),
        (near(near_q), near(near_doc), near(acc), near(top), near(total), *map(near, prevs)),
        attention_flops,
        4 * tokens * width,
    )

    def project(d, c0, cols, *after):
        out = pltpu.VMEM((tokens, cols), bf16)
        return call(
            lambda *refs: project_kernel(d, c0, *refs),
            [out, out],
            [VMEM] * 2 + [ANY] * len(after),
            (near(att), near(held), *after),
            4 * tokens * rows * cols,
            4 * rows * cols,
        )

    other_core = [(i, i ^ 1) for i in range(devices)]
    cols = block // HALVES
    parts = [[] for _ in range(HALVES)]
    after = []
    for d in list(range(1, chips)) + [0]:
        for c in range(HALVES):
            keep, give = project(d, c * cols, cols, *(after if d == 0 else []))
            got = lax.ppermute(give, "head", other_core)
            summed = keep.astype(f32) + got.astype(f32)
            if d > 0:
                pairs = [(i, (i + d * CORES) % devices) for i in range(devices)]
                summed = summed.astype(bf16)
                after = [summed]
                summed = lax.ppermute(summed, "head", pairs).astype(f32)
            parts[c].append(summed)
    outs = []
    for c in range(HALVES):
        result = parts[c][0]
        for part in parts[c][1:]:
            result = result + part
        outs.append(result.astype(bf16))
    return jnp.concatenate(outs, axis=1)


def solution(mesh):
    in_specs = (P("ctx", "head"), P("ctx", "head"), P("ctx", "head"), P("ctx"), P("head", None))
    out_specs = P("ctx", "head")
    return jax.shard_map(body, mesh=mesh, in_specs=in_specs, out_specs=out_specs, check_vma=False)
```

```python
import functools
import math

import jax
import jax.numpy as jnp
from jax import lax
from jax.experimental import pallas as pl
from jax.experimental.pallas import tpu as pltpu
from jax.sharding import PartitionSpec as P

HEAD_DIM = 128
CORES = 2
HALVES = 2
DOC_ROWS = 16
LOG2_SCALE = math.log2(math.e) / math.sqrt(HEAD_DIM)
HIDDEN = -1e30
NT = (((1,), (1,)), ((), ()))
VMEM = pl.BlockSpec(memory_space=pltpu.VMEM)
ANY = pl.BlockSpec(memory_space=pl.ANY)
HBM = pl.BlockSpec(memory_space=pltpu.HBM)


def near(x):
    return pltpu.with_memory_space_constraint(x, pltpu.VMEM)


def far(x):
    return pltpu.with_memory_space_constraint(x, pltpu.HBM)


def call(kernel, out_shape, in_specs, args, flops=0, moved=0, vmem_mib=32, scratch=()):
    return pl.pallas_call(
        kernel,
        out_shape=out_shape,
        in_specs=in_specs,
        out_specs=jax.tree.map(lambda _: VMEM, out_shape),
        scratch_shapes=scratch,
        compiler_params=pltpu.CompilerParams(vmem_limit_bytes=vmem_mib * 2**20),
        cost_estimate=pl.CostEstimate(
            flops=flops, bytes_accessed=moved, transcendentals=0
        ),
    )(*args)


def pack_kernel(k_hbm, v_hbm, doc_hbm, out_ref, held, sem):
    halves, size, width = out_ref.shape
    tokens = k_hbm.shape[0]
    rows = tokens // halves
    copies = [pltpu.make_async_copy(doc_hbm, held, sem.at[2 * halves])]
    for half in range(halves):
        for i, source in enumerate((k_hbm, v_hbm)):
            copies.append(
                pltpu.make_async_copy(
                    source.at[half * rows : (half + 1) * rows],
                    out_ref.at[half, i * rows : (i + 1) * rows],
                    sem.at[2 * half + i],
                )
            )
    for copy in copies:
        copy.start()
    copies[0].wait()
    docs = (held[...] + 1).astype(jnp.float32)
    for half in range(halves):
        parts = []
        for at in range(half * rows, (half + 1) * rows, width):
            part = docs[:, at : min(at + width, (half + 1) * rows)]
            if part.shape[1] < width:
                part = jnp.concatenate([part, jnp.zeros((1, width - part.shape[1]))], axis=1)
            parts.append(part)
        parts.append(jnp.zeros((DOC_ROWS - len(parts), width), jnp.float32))
        out_ref[half, 2 * rows :, :] = jnp.concatenate(parts, axis=0).astype(jnp.bfloat16)
    for copy in copies[1:]:
        copy.wait()


def doc_column(docs):
    count = docs.shape[1]
    return jnp.transpose(jnp.broadcast_to(docs, (count, count)))[:, :1]


def stacked(q_ref, r0, rows, first, repeats):
    heads = [
        q_ref[r0 : r0 + rows, h * HEAD_DIM : (h + 1) * HEAD_DIM]
        for h in range(first, first + repeats)
    ]
    return jnp.concatenate(heads, axis=0)


def with_ones(v):
    return jnp.concatenate([v, jnp.ones_like(v)], axis=1)


def hide(scores, bias):
    rows, count = bias.shape
    shape = (scores.shape[0] // rows, rows, count)
    return (scores.reshape(shape) + bias[None]).reshape(scores.shape)


def weights_of(scores, top):
    return jnp.exp2((scores - top) * LOG2_SCALE).astype(jnp.bfloat16)


def key_docs(ref, rows):
    wide = ref[2 * rows :, :].astype(jnp.float32)
    width = ref.shape[1]
    parts = [wide[i : i + 1, : min(width, rows)] for i in range(-(-rows // width))]
    return jnp.concatenate(parts, axis=1)


def attend(half, rows, q_ref, docs, own_k, own_v, prev_refs, att_ref):
    r0, count = half * rows, (half + 1) * rows
    groups = own_k.shape[1] // HEAD_DIM
    repeats = q_ref.shape[1] // HEAD_DIM // groups
    at = r0 + lax.broadcasted_iota(jnp.int32, (rows, count), 0)
    key = lax.broadcasted_iota(jnp.int32, (rows, count), 1)
    column = doc_column(docs)[r0 : r0 + rows]
    masks = [(key <= at) & (docs[:, :count] == column)]
    masks += [key_docs(prev, rows) == column for prev in prev_refs]
    bias = jnp.concatenate([jnp.where(mask, 0.0, HIDDEN) for mask in masks], axis=1)
    for g in range(groups):
        lanes = slice(g * HEAD_DIM, (g + 1) * HEAD_DIM)
        q = stacked(q_ref, r0, rows, g * repeats, repeats)
        k = jnp.concatenate([own_k[:count, lanes]] + [p[:rows, lanes] for p in prev_refs], axis=0)
        v = jnp.concatenate(
            [own_v[:count, lanes]] + [p[rows : 2 * rows, lanes] for p in prev_refs], axis=0
        )
        scores = lax.dot_general(q, k, NT, preferred_element_type=jnp.float32)
        scores = hide(scores, bias)
        top = jnp.max(scores, axis=1, keepdims=True)
        summed = jnp.dot(weights_of(scores, top), with_ones(v), preferred_element_type=jnp.float32)
        result = (summed[:, :HEAD_DIM] / summed[:, HEAD_DIM:]).astype(jnp.bfloat16)
        for r in range(repeats):
            h = g * repeats + r
            att_ref[:, h * HEAD_DIM : (h + 1) * HEAD_DIM] = result[r * rows : (r + 1) * rows]


def owner(d, which):
    chips = lax.axis_size("head") // CORES
    me = lax.axis_index("head")
    chip, core = me // CORES, me % CORES
    return lax.rem(chip + d, chips) * CORES + lax.rem(core + which, CORES)


def project(att, w_ref, d, which, out_ref):
    block = w_ref.shape[1] // lax.axis_size("head")
    start = pl.multiple_of(owner(d, which) * block, block)
    out_ref[...] = jnp.dot(
        att, w_ref[:, pl.ds(start, block)], preferred_element_type=jnp.float32
    ).astype(jnp.bfloat16)


def give_kernel(half, chips, q_ref, k_ref, v_ref, doc_ref, w_ref, *rest):
    outs = rest[-chips:]
    att_ref, gives = outs[0], outs[1:]
    prev_refs = rest[:-chips]
    if half < HALVES - 1:
        prev_refs = prev_refs[1:]
    rows = q_ref.shape[0] // HALVES
    docs = doc_ref[...].astype(jnp.float32) + 1.0
    attend(half, rows, q_ref, docs, k_ref, v_ref, prev_refs, att_ref)
    att = att_ref[...]
    for d in range(1, chips):
        project(att, w_ref, d, 1, gives[d - 1])


def keep_kernel(first, att_ref, w_ref, *outs):
    att = att_ref[...]
    for i, out_ref in enumerate(outs):
        project(att, w_ref, first + i, 0, out_ref)


def local_kernel(low_ref, high_ref, w_ref, after, give_ref, att_ref):
    rows = low_ref.shape[0]
    att_ref[:rows] = low_ref[...]
    att_ref[rows:] = high_ref[...]
    project(att_ref[...], w_ref, 0, 1, give_ref)


def sum_kernel(keep_ref, got_ref, out_ref):
    total = keep_ref[...].astype(jnp.float32) + got_ref[...].astype(jnp.float32)
    out_ref[...] = total.astype(out_ref.dtype)


def final_kernel(half, local_ref, *rest):
    out_hbm, held, sem = rest[-3:]
    arrived = rest[:-3] if half == HALVES - 1 else rest[:-4]
    rows = held.shape[0]
    here = pl.ds(half * rows, rows)
    total = local_ref[here, :]
    for got in arrived:
        total = total + got[...].astype(jnp.float32)
    held[...] = total.astype(jnp.bfloat16)
    copy = pltpu.make_async_copy(held, out_hbm.at[here], sem)
    copy.start()
    copy.wait()


def body(queries, keys, values, segment_ids, out_weight):
    tokens, width = queries.shape
    kv_width = keys.shape[1]
    place_count = lax.axis_size("ctx")
    devices = lax.axis_size("head")
    chips = devices // CORES
    columns = out_weight.shape[1]
    block = columns // devices
    span = max(place_count // 16, 2)
    part = tokens // HALVES
    bf16, f32 = jnp.bfloat16, jnp.float32
    dma = pltpu.SemaphoreType.DMA

    doc_row = segment_ids.reshape(1, tokens)
    packed = call(
        pack_kernel,
        pltpu.VMEM((HALVES, 2 * part + DOC_ROWS, kv_width), bf16),
        [HBM] * 3,
        (far(keys), far(values), far(doc_row)),
        flops=2**33,
        scratch=[pltpu.VMEM((1, tokens), jnp.int32), dma((2 * HALVES + 1,))],
    )
    late, early = [], []
    for s in range(1, span):
        pairs = [(i, i + s) for i in range(place_count - s)]
        late.append(lax.ppermute(packed[1], "ctx", pairs))
        early.append(lax.ppermute(packed[0], "ctx", pairs))

    other_core = [(i, i ^ 1) for i in range(devices)]

    def keep_shares(att, first, count):
        keep = pltpu.VMEM((att.shape[0], block), bf16)
        return call(
            functools.partial(keep_kernel, first),
            [keep] * count,
            [VMEM] * 2,
            (near(att), out_weight),
            flops=2**33,
        )

    def add(keep, got, dtype):
        return call(
            sum_kernel, pltpu.VMEM(keep.shape, dtype), [VMEM] * 2, (near(keep), near(got))
        )

    def shares(half, prevs, *after):
        att, *gives = call(
            functools.partial(give_kernel, half, chips),
            [pltpu.VMEM((part, width), bf16)] + [pltpu.VMEM((part, block), bf16)] * (chips - 1),
            [VMEM] * 5 + [ANY] * len(after) + [VMEM] * len(prevs),
            (queries, keys, values, doc_row, out_weight, *after, *map(near, prevs)),
            flops=8 * tokens * width * block,
        )
        keeps = keep_shares(att, 1, chips - 1)
        sums, arrived = [], []
        for d in range(1, chips):
            total = add(keeps[d - 1], lax.ppermute(gives[d - 1], "head", other_core), bf16)
            pairs = [(i, (i + d * CORES) % devices) for i in range(devices)]
            sums.append(total)
            arrived.append(lax.ppermute(total, "head", pairs))
        return att, sums, arrived

    att_high, sums, high = shares(HALVES - 1, early[:-1] + late)
    att_low, sums, low = shares(0, early + late, sums[-1])

    give, att = call(
        local_kernel,
        [pltpu.VMEM((tokens, block), bf16), pltpu.VMEM((tokens, width), bf16)],
        [VMEM] * 3 + [ANY],
        (near(att_low), near(att_high), out_weight, high[-1]),
        flops=4 * tokens * width * block,
    )
    (keep,) = keep_shares(att, 0, 1)
    local = add(keep, lax.ppermute(give, "head", other_core), f32)

    def finish(half, arrived, *out):
        return pl.pallas_call(
            functools.partial(final_kernel, half),
            out_shape=pltpu.HBM((tokens, block), bf16),
            in_specs=[VMEM] * (1 + len(arrived)) + [HBM] * len(out),
            out_specs=HBM,
            scratch_shapes=[pltpu.VMEM((part, block), bf16), dma],
            input_output_aliases={1 + len(arrived): 0} if out else {},
            cost_estimate=pl.CostEstimate(flops=0, bytes_accessed=0, transcendentals=0),
        )(near(local), *map(near, arrived), *out)

    return finish(0, low, finish(HALVES - 1, high))


def solution(mesh):
    in_specs = (P("ctx", "head"), P("ctx", "head"), P("ctx", "head"), P("ctx"), P("head", None))
    out_specs = P("ctx", "head")
    return jax.shard_map(body, mesh=mesh, in_specs=in_specs, out_specs=out_specs, check_vma=False)
```

```python
import functools
import math

import jax
import jax.numpy as jnp
from jax import lax
from jax.experimental import pallas as pl
from jax.experimental.pallas import tpu as pltpu
from jax.sharding import PartitionSpec as P

HEAD_DIM = 128
CORES = 2
CUT = 144 / 256
DOC_ROWS = 16
LOG2_SCALE = math.log2(math.e) / math.sqrt(HEAD_DIM)
HIDDEN = -1e30
NT = (((1,), (1,)), ((), ()))
VMEM = pl.BlockSpec(memory_space=pltpu.VMEM)
ANY = pl.BlockSpec(memory_space=pl.ANY)
HBM = pl.BlockSpec(memory_space=pltpu.HBM)


def near(x):
    return pltpu.with_memory_space_constraint(x, pltpu.VMEM)


def far(x):
    return pltpu.with_memory_space_constraint(x, pltpu.HBM)


def call(kernel, out_shape, in_specs, args, flops=0, moved=0, vmem_mib=32, scratch=()):
    return pl.pallas_call(
        kernel,
        out_shape=out_shape,
        in_specs=in_specs,
        out_specs=jax.tree.map(lambda _: VMEM, out_shape),
        scratch_shapes=scratch,
        compiler_params=pltpu.CompilerParams(vmem_limit_bytes=vmem_mib * 2**20),
        cost_estimate=pl.CostEstimate(
            flops=flops, bytes_accessed=moved, transcendentals=0
        ),
    )(*args)


def pack_kernel(k_hbm, v_hbm, doc_hbm, high_ref, held, sem):
    tokens, width = k_hbm.shape
    rows = (high_ref.shape[0] - DOC_ROWS) // 2
    copies = [pltpu.make_async_copy(doc_hbm, held, sem.at[2])]
    for i, source in enumerate((k_hbm, v_hbm)):
        copies.append(
            pltpu.make_async_copy(
                source.at[tokens - rows :], high_ref.at[i * rows : (i + 1) * rows], sem.at[i]
            )
        )
    for copy in copies:
        copy.start()
    copies[0].wait()
    docs = (held[...] + 1).astype(jnp.float32)
    parts = [docs[:, at : at + width] for at in range(0, tokens, width)]
    parts.append(jnp.zeros((DOC_ROWS - len(parts), width), jnp.float32))
    high_ref[2 * rows :, :] = jnp.concatenate(parts, axis=0).astype(jnp.bfloat16)
    for copy in copies[1:]:
        copy.wait()


def stacked(q_ref, r0, rows, first, repeats):
    heads = [
        q_ref[r0 : r0 + rows, h * HEAD_DIM : (h + 1) * HEAD_DIM]
        for h in range(first, first + repeats)
    ]
    return jnp.concatenate(heads, axis=0)


def with_ones(v):
    return jnp.concatenate([v, jnp.ones_like(v)], axis=1)


def hide(scores, bias):
    rows, count = bias.shape
    shape = (scores.shape[0] // rows, rows, count)
    return (scores.reshape(shape) + bias[None]).reshape(scores.shape)


def weights_of(scores, top):
    return jnp.exp2((scores - top) * LOG2_SCALE).astype(jnp.bfloat16)


def key_docs(high_ref, tokens):
    wide = high_ref[high_ref.shape[0] - DOC_ROWS :, :].astype(jnp.float32)
    parts = [wide[i : i + 1, :] for i in range(tokens // high_ref.shape[1])]
    return jnp.concatenate(parts, axis=1)


def attend(first, q_ref, bias_ref, column_ref, own_k, own_v, highs, lows, att_ref):
    tokens = q_ref.shape[0]
    rows = att_ref.shape[0]
    count = first + rows
    groups = own_k.shape[1] // HEAD_DIM
    repeats = q_ref.shape[1] // HEAD_DIM // groups
    column = column_ref[first:count, :]
    biases, keys, values = [], [], []
    for high, low in zip(highs, lows):
        n = (high.shape[0] - DOC_ROWS) // 2
        seen = tokens if low is not None else n
        if low is not None:
            keys.append(low[: tokens - n, :])
            values.append(low[tokens - n :, :])
        keys.append(high[:n, :])
        values.append(high[n : 2 * n, :])
        same = key_docs(high, tokens)[:, tokens - seen :] == column[:, :seen]
        biases.append(jnp.where(same, 0.0, HIDDEN))
    place = 0 if first else len(biases)
    biases.insert(place, bias_ref[first:count, :count])
    keys.insert(place * 2, own_k[:count, :])
    values.insert(place * 2, own_v[:count, :])
    bias = jnp.concatenate(biases, axis=1)
    all_keys = jnp.concatenate(keys, axis=0)
    all_values = jnp.concatenate(values, axis=0)
    lanes = [slice(g * HEAD_DIM, (g + 1) * HEAD_DIM) for g in range(groups)]
    queries = [stacked(q_ref, first, rows, g * repeats, repeats) for g in range(groups)]
    scores = [
        lax.dot_general(q, all_keys[:, at], NT, preferred_element_type=jnp.float32)
        for q, at in zip(queries, lanes)
    ]
    scores = [hide(s, bias) for s in scores]
    tops = [jnp.max(s, axis=1, keepdims=True) for s in scores]
    weights = [weights_of(s, top) for s, top in zip(scores, tops)]
    summed = [
        jnp.dot(w, with_ones(all_values[:, at]), preferred_element_type=jnp.float32)
        for w, at in zip(weights, lanes)
    ]
    for g in range(groups):
        result = (summed[g][:, :HEAD_DIM] / summed[g][:, HEAD_DIM:]).astype(jnp.bfloat16)
        for r in range(repeats):
            h = g * repeats + r
            att_ref[:, h * HEAD_DIM : (h + 1) * HEAD_DIM] = result[r * rows : (r + 1) * rows]


def mask_kernel(k_ref, v_ref, doc_ref, low_ref, bias_ref, column_ref):
    tokens = doc_ref.shape[1]
    cut = low_ref.shape[0] // 2
    low_ref[:cut] = k_ref[:cut]
    low_ref[cut:] = v_ref[:cut]
    docs = jnp.broadcast_to(doc_ref[...].astype(jnp.float32) + 1.0, (tokens, tokens))
    columns = jnp.transpose(docs)
    at = lax.broadcasted_iota(jnp.int32, (tokens, tokens), 0)
    key = lax.broadcasted_iota(jnp.int32, (tokens, tokens), 1)
    bias_ref[...] = jnp.where((key <= at) & (docs == columns), 0.0, HIDDEN)
    column_ref[...] = columns


def owner(d, which):
    chips = lax.axis_size("head") // CORES
    me = lax.axis_index("head")
    chip, core = me // CORES, me % CORES
    return lax.rem(chip + d, chips) * CORES + lax.rem(core + which, CORES)


def project(att, w_ref, d, which, out_ref):
    block = w_ref.shape[1] // lax.axis_size("head")
    start = pl.multiple_of(owner(d, which) * block, block)
    out_ref[...] = jnp.dot(
        att, w_ref[:, pl.ds(start, block)], preferred_element_type=jnp.float32
    ).astype(jnp.bfloat16)


def give_kernel(
    first, chips, n_high, n_low, q_ref, k_ref, v_ref, bias_ref, column_ref, w_ref, *rest
):
    outs = rest[-chips:]
    att_ref, gives = outs[0], outs[1:]
    highs, lows = list(rest[:n_high]), list(rest[n_high : n_high + n_low])
    lows += [None] * (n_high - n_low)
    here = lax.axis_index("ctx")

    def shares(highs, lows):
        attend(first, q_ref, bias_ref, column_ref, k_ref, v_ref, highs, lows, att_ref)
        att = att_ref[...]
        for d in range(1, chips):
            project(att, w_ref, d, 1, gives[d - 1])

    pl.when(here == 0)(lambda: shares([], []))
    pl.when(here > 0)(lambda: shares(highs, lows))


def keep_kernel(first, att_ref, w_ref, *outs):
    att = att_ref[...]
    for i, out_ref in enumerate(outs):
        project(att, w_ref, first + i, 0, out_ref)


def local_kernel(low_ref, high_ref, w_ref, after, att_ref, *gives):
    rows = low_ref.shape[0]
    att_ref[:rows] = low_ref[...]
    att_ref[rows:] = high_ref[...]
    block = w_ref.shape[1] // lax.axis_size("head")
    cols = block // len(gives)
    for i, give_ref in enumerate(gives):
        start = pl.multiple_of(owner(0, 1) * block + i * cols, cols)
        give_ref[...] = jnp.dot(
            att_ref[...], w_ref[:, pl.ds(start, cols)], preferred_element_type=jnp.float32
        ).astype(jnp.bfloat16)


def sum_kernel(keep_ref, *rest):
    out_ref, at = rest[-1], 0
    for got in rest[:-1]:
        lanes = slice(at, at + got.shape[1])
        total = keep_ref[:, lanes].astype(jnp.float32) + got[...].astype(jnp.float32)
        out_ref[:, lanes] = total.astype(out_ref.dtype)
        at += got.shape[1]


def final_kernel(first, count, local_ref, *rest):
    out_hbm, held, sem = rest[-3:]
    here = pl.ds(first, held.shape[0])
    total = local_ref[here, :]
    for got in rest[:count]:
        total = total + got[...].astype(jnp.float32)
    held[...] = total.astype(jnp.bfloat16)
    copy = pltpu.make_async_copy(held, out_hbm.at[here], sem)
    copy.start()
    copy.wait()


def body(queries, keys, values, segment_ids, out_weight):
    tokens, width = queries.shape
    kv_width = keys.shape[1]
    place_count = lax.axis_size("ctx")
    devices = lax.axis_size("head")
    chips = devices // CORES
    columns = out_weight.shape[1]
    block = columns // devices
    span = max(place_count // 16, 2)
    cut = int(tokens * CUT)
    bf16, f32 = jnp.bfloat16, jnp.float32
    dma = pltpu.SemaphoreType.DMA

    doc_row = segment_ids.reshape(1, tokens)
    groups = kv_width // HEAD_DIM
    packed_high = call(
        pack_kernel,
        pltpu.VMEM((2 * (tokens - cut) + DOC_ROWS, kv_width), bf16),
        [HBM] * 3,
        (far(keys), far(values), far(doc_row)),
        flops=2**33,
        scratch=[pltpu.VMEM((1, tokens), jnp.int32), dma((3,))],
    )
    packed_low, bias, column = call(
        mask_kernel,
        [
            pltpu.VMEM((2 * cut, kv_width), bf16),
            pltpu.VMEM((tokens, tokens), f32),
            pltpu.VMEM((tokens, tokens), f32),
        ],
        [VMEM] * 3,
        (keys, values, doc_row),
        flops=2**27,
    )
    highs, lows = [], []
    for s in range(1, span):
        line = [(i, i + s) for i in range(place_count - s)]
        ring = [(i, (i + s) % place_count) for i in range(place_count)]
        highs.append(lax.ppermute(packed_high, "ctx", line))
        lows.append(lax.ppermute(packed_low, "ctx", line))

    other_core = [(i, i ^ 1) for i in range(devices)]

    def keep_shares(att, first, count, flops):
        keep = pltpu.VMEM((att.shape[0], block), bf16)
        return call(
            functools.partial(keep_kernel, first),
            [keep] * count,
            [VMEM] * 2,
            (near(att), out_weight),
            flops=flops,
        )

    def add(keep, dtype, *got):
        return call(
            sum_kernel,
            pltpu.VMEM(keep.shape, dtype),
            [VMEM] * (1 + len(got)),
            tuple(map(near, (keep, *got))),
        )

    def shares(first, rows, lows, *after):
        prevs = highs + lows
        att, *gives = call(
            functools.partial(give_kernel, first, chips, len(highs), len(lows)),
            [pltpu.VMEM((rows, width), bf16)] + [pltpu.VMEM((rows, block), bf16)] * (chips - 1),
            [VMEM] * (6 + len(prevs)) + [ANY] * len(after),
            (
                *(queries, keys, values, near(bias), near(column), out_weight),
                *map(near, prevs),
                *after,
            ),
            flops=8 * tokens * width * block,
        )
        keeps = keep_shares(att, 1, chips - 1, 2**33)
        sums, arrived = [], []
        for d in range(1, chips):
            total = add(keeps[d - 1], bf16, lax.ppermute(gives[d - 1], "head", other_core))
            pairs = [(i, (i + d * CORES) % devices) for i in range(devices)]
            sums.append(total)
            arrived.append(lax.ppermute(total, "head", pairs))
        return att, sums, arrived

    att_high, sums, high = shares(cut, tokens - cut, lows[:-1])
    att_low, sums, low = shares(0, cut, lows, sums[-1])

    att, *gives = call(
        local_kernel,
        [pltpu.VMEM((tokens, width), bf16)] + [pltpu.VMEM((tokens, block // 2), bf16)] * 2,
        [VMEM] * 3 + [ANY],
        (near(att_low), near(att_high), out_weight, high[-1]),
        flops=4 * tokens * width * block,
    )
    (keep,) = keep_shares(att, 0, 1, 0)
    local = add(keep, f32, *[lax.ppermute(give, "head", other_core) for give in gives])

    def finish(first, rows, arrived, *out):
        return pl.pallas_call(
            functools.partial(final_kernel, first, len(arrived)),
            out_shape=pltpu.HBM((tokens, block), bf16),
            in_specs=[VMEM] * (1 + len(arrived)) + [HBM] * len(out),
            out_specs=HBM,
            scratch_shapes=[pltpu.VMEM((rows, block), bf16), dma],
            input_output_aliases={1 + len(arrived): 0} if out else {},
            cost_estimate=pl.CostEstimate(flops=0, bytes_accessed=0, transcendentals=0),
        )(near(local), *map(near, arrived), *out)

    return finish(0, cut, low, finish(cut, tokens - cut, high))


def solution(mesh):
    in_specs = (P("ctx", "head"), P("ctx", "head"), P("ctx", "head"), P("ctx"), P("head", None))
    out_specs = P("ctx", "head")
    return jax.shard_map(body, mesh=mesh, in_specs=in_specs, out_specs=out_specs, check_vma=False)
```

```python
import functools
import math

import jax
import jax.numpy as jnp
from jax import lax
from jax.experimental import pallas as pl
from jax.experimental.pallas import tpu as pltpu
from jax.sharding import PartitionSpec as P

HEAD_DIM = 128
CORES = 2
CUT = 160 / 256
DOC_ROWS = 16
LOG2_SCALE = math.log2(math.e) / math.sqrt(HEAD_DIM)
HIDDEN = -1e30
NT = (((1,), (1,)), ((), ()))
VMEM = pl.BlockSpec(memory_space=pltpu.VMEM)
ANY = pl.BlockSpec(memory_space=pl.ANY)
HBM = pl.BlockSpec(memory_space=pltpu.HBM)


def near(x):
    return pltpu.with_memory_space_constraint(x, pltpu.VMEM)


def far(x):
    return pltpu.with_memory_space_constraint(x, pltpu.HBM)


def call(kernel, out_shape, in_specs, args, flops=0, moved=0, vmem_mib=32, scratch=()):
    return pl.pallas_call(
        kernel,
        out_shape=out_shape,
        in_specs=in_specs,
        out_specs=jax.tree.map(lambda _: VMEM, out_shape),
        scratch_shapes=scratch,
        compiler_params=pltpu.CompilerParams(vmem_limit_bytes=vmem_mib * 2**20),
        cost_estimate=pl.CostEstimate(
            flops=flops, bytes_accessed=moved, transcendentals=0
        ),
    )(*args)


def pack_kernel(k_hbm, v_hbm, doc_hbm, high_ref, held, sem):
    tokens, width = k_hbm.shape
    rows = (high_ref.shape[0] - DOC_ROWS) // 2
    last = lax.axis_index("ctx") == lax.axis_size("ctx") - 1

    @pl.when(last)
    def _():
        high_ref[...] = jnp.zeros_like(high_ref)

    @pl.when(jnp.logical_not(last))
    def _():
        copies = [pltpu.make_async_copy(doc_hbm, held, sem.at[2])]
        for i, source in enumerate((k_hbm, v_hbm)):
            copies.append(
                pltpu.make_async_copy(
                    source.at[tokens - rows :], high_ref.at[i * rows : (i + 1) * rows], sem.at[i]
                )
            )
        for copy in copies:
            copy.start()
        copies[0].wait()
        docs = (held[...] + 1).astype(jnp.float32)
        parts = [docs[:, at : at + width] for at in range(0, tokens, width)]
        parts.append(jnp.zeros((DOC_ROWS - len(parts), width), jnp.float32))
        high_ref[2 * rows :, :] = jnp.concatenate(parts, axis=0).astype(jnp.bfloat16)
        for copy in copies[1:]:
            copy.wait()


def stacked(q_ref, r0, rows, first, repeats):
    heads = [
        q_ref[r0 : r0 + rows, h * HEAD_DIM : (h + 1) * HEAD_DIM]
        for h in range(first, first + repeats)
    ]
    return jnp.concatenate(heads, axis=0)


def with_ones(v):
    return jnp.concatenate([v, jnp.ones_like(v)], axis=1)


def hide(scores, bias):
    rows, count = bias.shape
    shape = (scores.shape[0] // rows, rows, count)
    return (scores.reshape(shape) + bias[None]).reshape(scores.shape)


def weights_of(scores, top):
    return jnp.exp2((scores - top) * LOG2_SCALE).astype(jnp.bfloat16)


def key_docs(high_ref, tokens):
    wide = high_ref[high_ref.shape[0] - DOC_ROWS :, :].astype(jnp.float32)
    parts = [wide[i : i + 1, :] for i in range(tokens // high_ref.shape[1])]
    return jnp.concatenate(parts, axis=1)


def attend(first, q_ref, bias_ref, column_ref, own_k, own_v, highs, lows, att_ref):
    tokens = q_ref.shape[0]
    rows = att_ref.shape[0]
    count = first + rows
    groups = own_k.shape[1] // HEAD_DIM
    repeats = q_ref.shape[1] // HEAD_DIM // groups
    column = column_ref[first:count, :]
    biases, keys, values = [], [], []
    for s, (high, low) in enumerate(zip(highs, lows), 1):
        n = (high.shape[0] - DOC_ROWS) // 2
        seen = tokens if low is not None else n
        if low is not None:
            keys.append(low[: tokens - n, :])
            values.append(low[tokens - n :, :])
        keys.append(high[:n, :])
        values.append(high[n : 2 * n, :])
        there = (lax.axis_index("ctx") >= s).astype(jnp.float32)
        same = key_docs(high, tokens)[:, tokens - seen :] * there == column[:, :seen]
        biases.append(jnp.where(same, 0.0, HIDDEN))
    place = 0 if first else len(biases)
    biases.insert(place, bias_ref[first:count, :count])
    keys.insert(place * 2, own_k[:count, :])
    values.insert(place * 2, own_v[:count, :])
    bias = jnp.concatenate(biases, axis=1)
    all_keys = jnp.concatenate(keys, axis=0)
    all_values = jnp.concatenate(values, axis=0)
    lanes = [slice(g * HEAD_DIM, (g + 1) * HEAD_DIM) for g in range(groups)]
    queries = [stacked(q_ref, first, rows, g * repeats, repeats) for g in range(groups)]
    scores = [
        lax.dot_general(q, all_keys[:, at], NT, preferred_element_type=jnp.float32)
        for q, at in zip(queries, lanes)
    ]
    scores = [hide(s, bias) for s in scores]
    tops = [jnp.max(s, axis=1, keepdims=True) for s in scores]
    weights = [weights_of(s, top) for s, top in zip(scores, tops)]
    summed = [
        jnp.dot(w, with_ones(all_values[:, at]), preferred_element_type=jnp.float32)
        for w, at in zip(weights, lanes)
    ]
    for g in range(groups):
        result = (summed[g][:, :HEAD_DIM] / summed[g][:, HEAD_DIM:]).astype(jnp.bfloat16)
        for r in range(repeats):
            h = g * repeats + r
            att_ref[:, h * HEAD_DIM : (h + 1) * HEAD_DIM] = result[r * rows : (r + 1) * rows]


def mask_kernel(k_ref, v_ref, doc_ref, low_ref, bias_ref, column_ref):
    tokens = doc_ref.shape[1]
    cut = low_ref.shape[0] // 2
    low_ref[:cut] = k_ref[:cut]
    low_ref[cut:] = v_ref[:cut]
    docs = jnp.broadcast_to(doc_ref[...].astype(jnp.float32) + 1.0, (tokens, tokens))
    columns = jnp.transpose(docs)
    at = lax.broadcasted_iota(jnp.int32, (tokens, tokens), 0)
    key = lax.broadcasted_iota(jnp.int32, (tokens, tokens), 1)
    bias_ref[...] = jnp.where((key <= at) & (docs == columns), 0.0, HIDDEN)
    column_ref[...] = columns


def owner(d, which):
    chips = lax.axis_size("head") // CORES
    me = lax.axis_index("head")
    chip, core = me // CORES, me % CORES
    return lax.rem(chip + d, chips) * CORES + lax.rem(core + which, CORES)


def project(att, w_ref, d, which, out_ref):
    block = w_ref.shape[1] // lax.axis_size("head")
    start = pl.multiple_of(owner(d, which) * block, block)
    out_ref[...] = jnp.dot(
        att, w_ref[:, pl.ds(start, block)], preferred_element_type=jnp.float32
    ).astype(jnp.bfloat16)


def give_shares(first, chips, refs, highs, lows, w_ref, att_ref, gives):
    attend(first, *refs, highs, lows, att_ref)
    att = att_ref[...]
    for d in range(1, chips):
        project(att, w_ref, d, 1, gives[d - 1])


def first_kernel(first, chips, q_ref, k_ref, v_ref, bias_ref, column_ref, w_ref, att_ref, *gives):
    @pl.when(lax.axis_index("ctx") == 0)
    def _():
        give_shares(first, chips, (q_ref, bias_ref, column_ref, k_ref, v_ref), [], [], w_ref, att_ref, gives)


def give_kernel(
    first, chips, n_high, n_low, n_done, q_ref, k_ref, v_ref, bias_ref, column_ref, w_ref, *rest
):
    outs = rest[-chips:]
    highs, lows = list(rest[:n_high]), list(rest[n_high : n_high + n_low])
    done = rest[n_high + n_low : n_high + n_low + n_done]
    lows += [None] * (n_high - n_low)
    refs = (q_ref, bias_ref, column_ref, k_ref, v_ref)
    here = lax.axis_index("ctx")

    @pl.when(here == 0)
    def _():
        if done:
            for ref, out in zip(done, outs):
                out[...] = ref[...]
        else:
            give_shares(first, chips, refs, [], [], w_ref, outs[0], outs[1:])

    @pl.when(here > 0)
    def _():
        give_shares(first, chips, refs, highs, lows, w_ref, outs[0], outs[1:])


def keep_kernel(first, att_ref, w_ref, *outs):
    att = att_ref[...]
    for i, out_ref in enumerate(outs):
        project(att, w_ref, first + i, 0, out_ref)


def local_kernel(low_ref, high_ref, w_ref, after, att_ref, *gives):
    rows = low_ref.shape[0]
    att_ref[:rows] = low_ref[...]
    att_ref[rows:] = high_ref[...]
    block = w_ref.shape[1] // lax.axis_size("head")
    cols = block // len(gives)
    for i, give_ref in enumerate(gives):
        start = pl.multiple_of(owner(0, 1) * block + i * cols, cols)
        give_ref[...] = jnp.dot(
            att_ref[...], w_ref[:, pl.ds(start, cols)], preferred_element_type=jnp.float32
        ).astype(jnp.bfloat16)


def sum_kernel(keep_ref, *rest):
    out_ref, at = rest[-1], 0
    for got in rest[:-1]:
        lanes = slice(at, at + got.shape[1])
        total = keep_ref[:, lanes].astype(jnp.float32) + got[...].astype(jnp.float32)
        out_ref[:, lanes] = total.astype(out_ref.dtype)
        at += got.shape[1]


def final_kernel(first, count, local_ref, *rest):
    out_hbm, held, sem = rest[-3:]
    here = pl.ds(first, held.shape[0])
    total = local_ref[here, :]
    for got in rest[:count]:
        total = total + got[...].astype(jnp.float32)
    held[...] = total.astype(jnp.bfloat16)
    copy = pltpu.make_async_copy(held, out_hbm.at[here], sem)
    copy.start()
    copy.wait()


def body(queries, keys, values, segment_ids, out_weight):
    tokens, width = queries.shape
    kv_width = keys.shape[1]
    place_count = lax.axis_size("ctx")
    devices = lax.axis_size("head")
    chips = devices // CORES
    columns = out_weight.shape[1]
    block = columns // devices
    span = max(place_count // 16, 2)
    cut = int(tokens * CUT)
    bf16, f32 = jnp.bfloat16, jnp.float32
    dma = pltpu.SemaphoreType.DMA

    doc_row = segment_ids.reshape(1, tokens)
    groups = kv_width // HEAD_DIM
    packed_high = call(
        pack_kernel,
        pltpu.VMEM((2 * (tokens - cut) + DOC_ROWS, kv_width), bf16),
        [HBM] * 3,
        (far(keys), far(values), far(doc_row)),
        flops=2**33,
        scratch=[pltpu.VMEM((1, tokens), jnp.int32), dma((3,))],
    )
    packed_low, bias, column = call(
        mask_kernel,
        [
            pltpu.VMEM((2 * cut, kv_width), bf16),
            pltpu.VMEM((tokens, tokens), f32),
            pltpu.VMEM((tokens, tokens), f32),
        ],
        [VMEM] * 3,
        (keys, values, doc_row),
        flops=2**27,
    )
    highs, lows = [], []
    for s in range(1, span):
        ring = [(i, (i + s) % place_count) for i in range(place_count)]
        highs.append(lax.ppermute(packed_high, "ctx", ring))
        lows.append(lax.ppermute(packed_low, "ctx", ring[: place_count - s]))

    other_core = [(i, i ^ 1) for i in range(devices)]

    def keep_shares(att, first, count, flops):
        keep = pltpu.VMEM((att.shape[0], block), bf16)
        return call(
            functools.partial(keep_kernel, first),
            [keep] * count,
            [VMEM] * 2,
            (near(att), out_weight),
            flops=flops,
        )

    def add(keep, dtype, *got):
        return call(
            sum_kernel,
            pltpu.VMEM(keep.shape, dtype),
            [VMEM] * (1 + len(got)),
            tuple(map(near, (keep, *got))),
        )

    def outputs(rows):
        return [pltpu.VMEM((rows, width), bf16)] + [pltpu.VMEM((rows, block), bf16)] * (chips - 1)

    always = (queries, keys, values, near(bias), near(column), out_weight)
    done = call(
        functools.partial(first_kernel, cut, chips),
        outputs(tokens - cut),
        [VMEM] * len(always),
        always,
        flops=2**27,
    )

    def shares(first, rows, lows, done, *after):
        prevs = highs + lows + done
        att, *gives = call(
            functools.partial(give_kernel, first, chips, len(highs), len(lows), len(done)),
            outputs(rows),
            [VMEM] * (len(always) + len(prevs)) + [ANY] * len(after),
            (*always, *map(near, prevs), *after),
            flops=8 * tokens * width * block,
        )
        keeps = keep_shares(att, 1, chips - 1, 2**33)
        sums, arrived = [], []
        for d in range(1, chips):
            total = add(keeps[d - 1], bf16, lax.ppermute(gives[d - 1], "head", other_core))
            pairs = [(i, (i + d * CORES) % devices) for i in range(devices)]
            sums.append(total)
            arrived.append(lax.ppermute(total, "head", pairs))
        return att, sums, arrived

    att_high, sums, high = shares(cut, tokens - cut, lows[:-1], list(done))
    att_low, sums, low = shares(0, cut, lows, [], sums[-1])

    att, *gives = call(
        local_kernel,
        [pltpu.VMEM((tokens, width), bf16)] + [pltpu.VMEM((tokens, block // 2), bf16)] * 2,
        [VMEM] * 3 + [ANY],
        (near(att_low), near(att_high), out_weight, high[-1]),
        flops=4 * tokens * width * block,
    )
    (keep,) = keep_shares(att, 0, 1, 0)
    local = add(keep, f32, *[lax.ppermute(give, "head", other_core) for give in gives])

    def finish(first, rows, arrived, *out):
        return pl.pallas_call(
            functools.partial(final_kernel, first, len(arrived)),
            out_shape=pltpu.HBM((tokens, block), bf16),
            in_specs=[VMEM] * (1 + len(arrived)) + [HBM] * len(out),
            out_specs=HBM,
            scratch_shapes=[pltpu.VMEM((rows, block), bf16), dma],
            input_output_aliases={1 + len(arrived): 0} if out else {},
            cost_estimate=pl.CostEstimate(flops=0, bytes_accessed=0, transcendentals=0),
        )(near(local), *map(near, arrived), *out)

    return finish(0, cut, low, finish(cut, tokens - cut, high))


def solution(mesh):
    in_specs = (P("ctx", "head"), P("ctx", "head"), P("ctx", "head"), P("ctx"), P("head", None))
    out_specs = P("ctx", "head")
    return jax.shard_map(body, mesh=mesh, in_specs=in_specs, out_specs=out_specs, check_vma=False)
```

```python
import functools
import math

import jax
import jax.numpy as jnp
from jax import lax
from jax.experimental import pallas as pl
from jax.experimental.pallas import tpu as pltpu
from jax.sharding import PartitionSpec as P

HEAD_DIM = 128
CORES = 2
CUT = 160 / 256
DOC_ROWS = 16
LOG2_SCALE = math.log2(math.e) / math.sqrt(HEAD_DIM)
HIDDEN = -1e30
NT = (((1,), (1,)), ((), ()))
VMEM = pl.BlockSpec(memory_space=pltpu.VMEM)
ANY = pl.BlockSpec(memory_space=pl.ANY)
HBM = pl.BlockSpec(memory_space=pltpu.HBM)


def near(x):
    return pltpu.with_memory_space_constraint(x, pltpu.VMEM)


def far(x):
    return pltpu.with_memory_space_constraint(x, pltpu.HBM)


def call(kernel, out_shape, in_specs, args, flops=0, moved=0, vmem_mib=32, scratch=()):
    return pl.pallas_call(
        kernel,
        out_shape=out_shape,
        in_specs=in_specs,
        out_specs=jax.tree.map(lambda _: VMEM, out_shape),
        scratch_shapes=scratch,
        compiler_params=pltpu.CompilerParams(vmem_limit_bytes=vmem_mib * 2**20),
        cost_estimate=pl.CostEstimate(
            flops=flops, bytes_accessed=moved, transcendentals=0
        ),
    )(*args)


def pack_kernel(k_hbm, v_hbm, doc_hbm, high_ref, held, sem):
    tokens, width = k_hbm.shape
    rows = (high_ref.shape[0] - DOC_ROWS) // 2
    last = lax.axis_index("ctx") == lax.axis_size("ctx") - 1

    @pl.when(last)
    def _():
        high_ref[...] = jnp.zeros_like(high_ref)

    @pl.when(jnp.logical_not(last))
    def _():
        copies = [pltpu.make_async_copy(doc_hbm, held, sem.at[2])]
        for i, source in enumerate((k_hbm, v_hbm)):
            copies.append(
                pltpu.make_async_copy(
                    source.at[tokens - rows :], high_ref.at[i * rows : (i + 1) * rows], sem.at[i]
                )
            )
        for copy in copies:
            copy.start()
        copies[0].wait()
        docs = (held[...] + 1).astype(jnp.float32)
        parts = [docs[:, at : at + width] for at in range(0, tokens, width)]
        parts.append(jnp.zeros((DOC_ROWS - len(parts), width), jnp.float32))
        high_ref[2 * rows :, :] = jnp.concatenate(parts, axis=0).astype(jnp.bfloat16)
        for copy in copies[1:]:
            copy.wait()


def stacked(q_ref, r0, rows, first, repeats):
    heads = [
        q_ref[r0 : r0 + rows, h * HEAD_DIM : (h + 1) * HEAD_DIM]
        for h in range(first, first + repeats)
    ]
    return jnp.concatenate(heads, axis=0)


def with_ones(v):
    return jnp.concatenate([v, jnp.ones_like(v)], axis=1)


def hide(scores, bias):
    rows, count = bias.shape
    shape = (scores.shape[0] // rows, rows, count)
    return (scores.reshape(shape) + bias[None]).reshape(scores.shape)


def weights_of(scores, top):
    return jnp.exp2((scores - top) * LOG2_SCALE).astype(jnp.bfloat16)


def key_docs(high_ref, tokens):
    wide = high_ref[high_ref.shape[0] - DOC_ROWS :, :].astype(jnp.float32)
    parts = [wide[i : i + 1, :] for i in range(tokens // high_ref.shape[1])]
    return jnp.concatenate(parts, axis=1)


def attend(first, q_ref, bias_ref, column_ref, own_k, own_v, highs, lows, att_ref):
    tokens = q_ref.shape[0]
    rows = att_ref.shape[0]
    count = first + rows
    groups = own_k.shape[1] // HEAD_DIM
    repeats = q_ref.shape[1] // HEAD_DIM // groups
    column = column_ref[first:count, :]
    biases, keys, values = [], [], []
    for s, (high, low) in enumerate(zip(highs, lows), 1):
        n = (high.shape[0] - DOC_ROWS) // 2
        seen = tokens if low is not None else n
        if low is not None:
            keys.append(low[: tokens - n, :])
            values.append(low[tokens - n :, :])
        keys.append(high[:n, :])
        values.append(high[n : 2 * n, :])
        there = (lax.axis_index("ctx") >= s).astype(jnp.float32)
        same = key_docs(high, tokens)[:, tokens - seen :] * there == column[:, :seen]
        biases.append(jnp.where(same, 0.0, HIDDEN))
    place = 0 if first else len(biases)
    biases.insert(place, bias_ref[first:count, :count])
    keys.insert(place * 2, own_k[:count, :])
    values.insert(place * 2, own_v[:count, :])
    bias = jnp.concatenate(biases, axis=1)
    all_keys = jnp.concatenate(keys, axis=0)
    all_values = jnp.concatenate(values, axis=0)
    lanes = [slice(g * HEAD_DIM, (g + 1) * HEAD_DIM) for g in range(groups)]
    queries = [stacked(q_ref, first, rows, g * repeats, repeats) for g in range(groups)]
    scores = [
        lax.dot_general(q, all_keys[:, at], NT, preferred_element_type=jnp.float32)
        for q, at in zip(queries, lanes)
    ]
    scores = [hide(s, bias) for s in scores]
    tops = [jnp.max(s, axis=1, keepdims=True) for s in scores]
    weights = [weights_of(s, top) for s, top in zip(scores, tops)]
    summed = [
        jnp.dot(w, with_ones(all_values[:, at]), preferred_element_type=jnp.float32)
        for w, at in zip(weights, lanes)
    ]
    for g in range(groups):
        result = (summed[g][:, :HEAD_DIM] / summed[g][:, HEAD_DIM:]).astype(jnp.bfloat16)
        for r in range(repeats):
            h = g * repeats + r
            att_ref[:, h * HEAD_DIM : (h + 1) * HEAD_DIM] = result[r * rows : (r + 1) * rows]


def mask_kernel(k_ref, v_ref, doc_ref, low_ref, bias_ref, column_ref):
    tokens = doc_ref.shape[1]
    cut = low_ref.shape[0] // 2
    low_ref[:cut] = k_ref[:cut]
    low_ref[cut:] = v_ref[:cut]
    docs = jnp.broadcast_to(doc_ref[...].astype(jnp.float32) + 1.0, (tokens, tokens))
    columns = jnp.transpose(docs)
    at = lax.broadcasted_iota(jnp.int32, (tokens, tokens), 0)
    key = lax.broadcasted_iota(jnp.int32, (tokens, tokens), 1)
    bias_ref[...] = jnp.where((key <= at) & (docs == columns), 0.0, HIDDEN)
    column_ref[...] = columns


def owner(d, which):
    chips = lax.axis_size("head") // CORES
    me = lax.axis_index("head")
    chip, core = me // CORES, me % CORES
    return lax.rem(chip + d, chips) * CORES + lax.rem(core + which, CORES)


def project(att, w_ref, d, which, out_ref):
    block = w_ref.shape[1] // lax.axis_size("head")
    start = pl.multiple_of(owner(d, which) * block, block)
    out_ref[...] = jnp.dot(
        att, w_ref[:, pl.ds(start, block)], preferred_element_type=jnp.float32
    ).astype(jnp.bfloat16)


def give_shares(first, chips, refs, highs, lows, w_ref, att_ref, gives):
    attend(first, *refs, highs, lows, att_ref)
    att = att_ref[...]
    for d in range(1, chips):
        project(att, w_ref, d, 1, gives[d - 1])


def first_kernel(cut, chips, q_ref, k_ref, v_ref, bias_ref, column_ref, w_ref, *outs):
    refs = (q_ref, bias_ref, column_ref, k_ref, v_ref)
    highs, lows = outs[:chips], outs[chips:]

    @pl.when(lax.axis_index("ctx") == 0)
    def _():
        for first, (att_ref, *gives) in ((cut, highs), (0, lows)):
            give_shares(first, chips, refs, [], [], w_ref, att_ref, gives)


def give_kernel(
    first, chips, n_high, n_low, q_ref, k_ref, v_ref, bias_ref, column_ref, w_ref, *rest
):
    outs = rest[-chips:]
    highs, lows = list(rest[:n_high]), list(rest[n_high : n_high + n_low])
    done = rest[n_high + n_low : n_high + n_low + chips]
    lows += [None] * (n_high - n_low)
    refs = (q_ref, bias_ref, column_ref, k_ref, v_ref)
    here = lax.axis_index("ctx")

    @pl.when(here == 0)
    def _():
        for ref, out in zip(done, outs):
            out[...] = ref[...]

    @pl.when(here > 0)
    def _():
        give_shares(first, chips, refs, highs, lows, w_ref, outs[0], outs[1:])


def keep_kernel(first, att_ref, w_ref, *outs):
    att = att_ref[...]
    for i, out_ref in enumerate(outs):
        project(att, w_ref, first + i, 0, out_ref)


def local_kernel(low_ref, high_ref, w_ref, after, att_ref, *gives):
    rows = low_ref.shape[0]
    att_ref[:rows] = low_ref[...]
    att_ref[rows:] = high_ref[...]
    block = w_ref.shape[1] // lax.axis_size("head")
    cols = block // len(gives)
    for i, give_ref in enumerate(gives):
        start = pl.multiple_of(owner(0, 1) * block + i * cols, cols)
        give_ref[...] = jnp.dot(
            att_ref[...], w_ref[:, pl.ds(start, cols)], preferred_element_type=jnp.float32
        ).astype(jnp.bfloat16)


def sum_kernel(keep_ref, *rest):
    out_ref, at = rest[-1], 0
    for got in rest[:-1]:
        lanes = slice(at, at + got.shape[1])
        total = keep_ref[:, lanes].astype(jnp.float32) + got[...].astype(jnp.float32)
        out_ref[:, lanes] = total.astype(out_ref.dtype)
        at += got.shape[1]


def final_kernel(first, count, local_ref, *rest):
    out_hbm, held, sem = rest[-3:]
    here = pl.ds(first, held.shape[0])
    total = local_ref[here, :]
    for got in rest[:count]:
        total = total + got[...].astype(jnp.float32)
    held[...] = total.astype(jnp.bfloat16)
    copy = pltpu.make_async_copy(held, out_hbm.at[here], sem)
    copy.start()
    copy.wait()


def body(queries, keys, values, segment_ids, out_weight):
    tokens, width = queries.shape
    kv_width = keys.shape[1]
    place_count = lax.axis_size("ctx")
    devices = lax.axis_size("head")
    chips = devices // CORES
    columns = out_weight.shape[1]
    block = columns // devices
    span = max(place_count // 16, 2)
    cut = int(tokens * CUT)
    bf16, f32 = jnp.bfloat16, jnp.float32
    dma = pltpu.SemaphoreType.DMA

    doc_row = segment_ids.reshape(1, tokens)
    groups = kv_width // HEAD_DIM
    packed_high = call(
        pack_kernel,
        pltpu.VMEM((2 * (tokens - cut) + DOC_ROWS, kv_width), bf16),
        [HBM] * 3,
        (far(keys), far(values), far(doc_row)),
        flops=2**33,
        scratch=[pltpu.VMEM((1, tokens), jnp.int32), dma((3,))],
    )
    packed_low, bias, column = call(
        mask_kernel,
        [
            pltpu.VMEM((2 * cut, kv_width), bf16),
            pltpu.VMEM((tokens, tokens), f32),
            pltpu.VMEM((tokens, tokens), f32),
        ],
        [VMEM] * 3,
        (keys, values, doc_row),
        flops=2**27,
    )
    highs, lows = [], []
    for s in range(1, span):
        ring = [(i, (i + s) % place_count) for i in range(place_count)]
        highs.append(lax.ppermute(packed_high, "ctx", ring))
        lows.append(lax.ppermute(packed_low, "ctx", ring[: place_count - s]))

    other_core = [(i, i ^ 1) for i in range(devices)]

    def keep_shares(att, first, count, flops):
        keep = pltpu.VMEM((att.shape[0], block), bf16)
        return call(
            functools.partial(keep_kernel, first),
            [keep] * count,
            [VMEM] * 2,
            (near(att), out_weight),
            flops=flops,
        )

    def add(keep, dtype, *got):
        return call(
            sum_kernel,
            pltpu.VMEM(keep.shape, dtype),
            [VMEM] * (1 + len(got)),
            tuple(map(near, (keep, *got))),
        )

    def outputs(rows):
        return [pltpu.VMEM((rows, width), bf16)] + [pltpu.VMEM((rows, block), bf16)] * (chips - 1)

    always = (queries, keys, values, near(bias), near(column), out_weight)
    done = call(
        functools.partial(first_kernel, cut, chips),
        outputs(tokens - cut) + outputs(cut),
        [VMEM] * len(always),
        always,
        flops=2**27,
    )

    def shares(first, rows, lows, done, *after):
        prevs = highs + lows + done
        att, *gives = call(
            functools.partial(give_kernel, first, chips, len(highs), len(lows)),
            outputs(rows),
            [VMEM] * (len(always) + len(prevs)) + [ANY] * len(after),
            (*always, *map(near, prevs), *after),
            flops=8 * tokens * width * block,
        )
        keeps = keep_shares(att, 1, chips - 1, 2**33)
        sums, arrived = [], []
        for d in range(1, chips):
            total = add(keeps[d - 1], bf16, lax.ppermute(gives[d - 1], "head", other_core))
            pairs = [(i, (i + d * CORES) % devices) for i in range(devices)]
            sums.append(total)
            arrived.append(lax.ppermute(total, "head", pairs))
        return att, sums, arrived

    att_high, sums, high = shares(cut, tokens - cut, lows[:-1], list(done[:chips]))
    att_low, sums, low = shares(0, cut, lows, list(done[chips:]), sums[-1])

    att, *gives = call(
        local_kernel,
        [pltpu.VMEM((tokens, width), bf16)] + [pltpu.VMEM((tokens, block // 2), bf16)] * 2,
        [VMEM] * 3 + [ANY],
        (near(att_low), near(att_high), out_weight, high[-1]),
        flops=4 * tokens * width * block,
    )
    (keep,) = keep_shares(att, 0, 1, 0)
    local = add(keep, f32, *[lax.ppermute(give, "head", other_core) for give in gives])

    def finish(first, rows, arrived, *out):
        return pl.pallas_call(
            functools.partial(final_kernel, first, len(arrived)),
            out_shape=pltpu.HBM((tokens, block), bf16),
            in_specs=[VMEM] * (1 + len(arrived)) + [HBM] * len(out),
            out_specs=HBM,
            scratch_shapes=[pltpu.VMEM((rows, block), bf16), dma],
            input_output_aliases={1 + len(arrived): 0} if out else {},
            cost_estimate=pl.CostEstimate(flops=0, bytes_accessed=0, transcendentals=0),
        )(near(local), *map(near, arrived), *out)

    return finish(0, cut, low, finish(cut, tokens - cut, high))


def solution(mesh):
    in_specs = (P("ctx", "head"), P("ctx", "head"), P("ctx", "head"), P("ctx"), P("head", None))
    out_specs = P("ctx", "head")
    return jax.shard_map(body, mesh=mesh, in_specs=in_specs, out_specs=out_specs, check_vma=False)
```

```python
import functools
import math

import jax
import jax.numpy as jnp
from jax import lax
from jax.experimental import pallas as pl
from jax.experimental.pallas import tpu as pltpu
from jax.sharding import PartitionSpec as P

HEAD_DIM = 128
CORES = 2
CUT = 160 / 256
DOC_ROWS = 16
PIECES = 2
LOG2_SCALE = math.log2(math.e) / math.sqrt(HEAD_DIM)
HIDDEN = -1e30
NT = (((1,), (1,)), ((), ()))
VMEM = pl.BlockSpec(memory_space=pltpu.VMEM)
ANY = pl.BlockSpec(memory_space=pl.ANY)
HBM = pl.BlockSpec(memory_space=pltpu.HBM)


def near(x):
    return pltpu.with_memory_space_constraint(x, pltpu.VMEM)


def far(x):
    return pltpu.with_memory_space_constraint(x, pltpu.HBM)


def call(kernel, out_shape, in_specs, args, flops=0, moved=0, vmem_mib=32, scratch=()):
    return pl.pallas_call(
        kernel,
        out_shape=out_shape,
        in_specs=in_specs,
        out_specs=jax.tree.map(lambda _: VMEM, out_shape),
        scratch_shapes=scratch,
        compiler_params=pltpu.CompilerParams(vmem_limit_bytes=vmem_mib * 2**20),
        cost_estimate=pl.CostEstimate(
            flops=flops, bytes_accessed=moved, transcendentals=0
        ),
    )(*args)


def pack_kernel(k_hbm, v_hbm, doc_hbm, high_ref, held, sem):
    tokens, width = k_hbm.shape
    rows = (high_ref.shape[0] - DOC_ROWS) // 2
    last = lax.axis_index("ctx") == lax.axis_size("ctx") - 1

    @pl.when(last)
    def _():
        high_ref[...] = jnp.zeros_like(high_ref)

    @pl.when(jnp.logical_not(last))
    def _():
        copies = [pltpu.make_async_copy(doc_hbm, held, sem.at[2])]
        for i, source in enumerate((k_hbm, v_hbm)):
            copies.append(
                pltpu.make_async_copy(
                    source.at[tokens - rows :], high_ref.at[i * rows : (i + 1) * rows], sem.at[i]
                )
            )
        for copy in copies:
            copy.start()
        copies[0].wait()
        docs = (held[...] + 1).astype(jnp.float32)
        parts = [docs[:, at : at + width] for at in range(0, tokens, width)]
        parts.append(jnp.zeros((DOC_ROWS - len(parts), width), jnp.float32))
        high_ref[2 * rows :, :] = jnp.concatenate(parts, axis=0).astype(jnp.bfloat16)
        for copy in copies[1:]:
            copy.wait()


def stacked(q_ref, r0, rows, first, repeats):
    heads = [
        q_ref[r0 : r0 + rows, h * HEAD_DIM : (h + 1) * HEAD_DIM]
        for h in range(first, first + repeats)
    ]
    return jnp.concatenate(heads, axis=0)


def with_ones(v):
    return jnp.concatenate([v, jnp.ones_like(v)], axis=1)


def hide(scores, bias):
    rows, count = bias.shape
    shape = (scores.shape[0] // rows, rows, count)
    return (scores.reshape(shape) + bias[None]).reshape(scores.shape)


def weights_of(scores, top):
    return jnp.exp2((scores - top) * LOG2_SCALE).astype(jnp.bfloat16)


def key_docs(high_ref, tokens):
    wide = high_ref[high_ref.shape[0] - DOC_ROWS :, :].astype(jnp.float32)
    parts = [wide[i : i + 1, :] for i in range(tokens // high_ref.shape[1])]
    return jnp.concatenate(parts, axis=1)


def attend(first, q_ref, bias_ref, column_ref, own_k, own_v, highs, lows, att_ref):
    tokens = q_ref.shape[0]
    rows = att_ref.shape[0]
    count = first + rows
    groups = own_k.shape[1] // HEAD_DIM
    repeats = q_ref.shape[1] // HEAD_DIM // groups
    column = column_ref[first:count, :]
    biases, keys, values = [], [], []
    for s, (high, low) in enumerate(zip(highs, lows), 1):
        n = (high.shape[0] - DOC_ROWS) // 2
        seen = tokens if low is not None else n
        if low is not None:
            keys.append(low[: tokens - n, :])
            values.append(low[tokens - n :, :])
        keys.append(high[:n, :])
        values.append(high[n : 2 * n, :])
        there = (lax.axis_index("ctx") >= s).astype(jnp.float32)
        same = key_docs(high, tokens)[:, tokens - seen :] * there == column[:, :seen]
        biases.append(jnp.where(same, 0.0, HIDDEN))
    place = 0 if first else len(biases)
    biases.insert(place, bias_ref[first:count, :count])
    keys.insert(place * 2, own_k[:count, :])
    values.insert(place * 2, own_v[:count, :])
    bias = jnp.concatenate(biases, axis=1)
    all_keys = jnp.concatenate(keys, axis=0)
    all_values = jnp.concatenate(values, axis=0)
    lanes = [slice(g * HEAD_DIM, (g + 1) * HEAD_DIM) for g in range(groups)]
    queries = [stacked(q_ref, first, rows, g * repeats, repeats) for g in range(groups)]
    scores = [
        lax.dot_general(q, all_keys[:, at], NT, preferred_element_type=jnp.float32)
        for q, at in zip(queries, lanes)
    ]
    scores = [hide(s, bias) for s in scores]
    tops = [jnp.max(s, axis=1, keepdims=True) for s in scores]
    weights = [weights_of(s, top) for s, top in zip(scores, tops)]
    summed = [
        jnp.dot(w, with_ones(all_values[:, at]), preferred_element_type=jnp.float32)
        for w, at in zip(weights, lanes)
    ]
    for g in range(groups):
        result = (summed[g][:, :HEAD_DIM] / summed[g][:, HEAD_DIM:]).astype(jnp.bfloat16)
        for r in range(repeats):
            h = g * repeats + r
            att_ref[:, h * HEAD_DIM : (h + 1) * HEAD_DIM] = result[r * rows : (r + 1) * rows]


def mask_kernel(k_ref, v_ref, doc_ref, low_ref, bias_ref, column_ref):
    tokens = doc_ref.shape[1]
    cut = low_ref.shape[0] // 2
    low_ref[:cut] = k_ref[:cut]
    low_ref[cut:] = v_ref[:cut]
    docs = jnp.broadcast_to(doc_ref[...].astype(jnp.float32) + 1.0, (tokens, tokens))
    columns = jnp.transpose(docs)
    at = lax.broadcasted_iota(jnp.int32, (tokens, tokens), 0)
    key = lax.broadcasted_iota(jnp.int32, (tokens, tokens), 1)
    bias_ref[...] = jnp.where((key <= at) & (docs == columns), 0.0, HIDDEN)
    column_ref[...] = columns


def owner(d, which):
    chips = lax.axis_size("head") // CORES
    me = lax.axis_index("head")
    chip, core = me // CORES, me % CORES
    return lax.rem(chip + d, chips) * CORES + lax.rem(core + which, CORES)


def project(att, w_ref, d, which, out_refs):
    block = w_ref.shape[1] // lax.axis_size("head")
    start = pl.multiple_of(owner(d, which) * block, block)
    share = jnp.dot(att, w_ref[:, pl.ds(start, block)], preferred_element_type=jnp.float32)
    cols = block // len(out_refs)
    for i, ref in enumerate(out_refs):
        ref[...] = share[:, i * cols : (i + 1) * cols].astype(jnp.bfloat16)


def give_shares(first, chips, refs, highs, lows, w_ref, att_ref, gives):
    attend(first, *refs, highs, lows, att_ref)
    att = att_ref[...]
    pieces = len(gives) // (chips - 1)
    for d in range(1, chips):
        project(att, w_ref, d, 1, gives[(d - 1) * pieces : d * pieces])


def first_kernel(cut, chips, n_outs, q_ref, k_ref, v_ref, bias_ref, column_ref, w_ref, *outs):
    refs = (q_ref, bias_ref, column_ref, k_ref, v_ref)
    highs, lows = outs[:n_outs], outs[n_outs:]

    @pl.when(lax.axis_index("ctx") == 0)
    def _():
        for first, (att_ref, *gives) in ((cut, highs), (0, lows)):
            give_shares(first, chips, refs, [], [], w_ref, att_ref, gives)


def give_kernel(
    first, chips, n_outs, n_high, n_low, q_ref, k_ref, v_ref, bias_ref, column_ref, w_ref, *rest
):
    outs = rest[-n_outs:]
    highs, lows = list(rest[:n_high]), list(rest[n_high : n_high + n_low])
    done = rest[n_high + n_low : n_high + n_low + n_outs]
    lows += [None] * (n_high - n_low)
    refs = (q_ref, bias_ref, column_ref, k_ref, v_ref)
    here = lax.axis_index("ctx")

    @pl.when(here == 0)
    def _():
        for ref, out in zip(done, outs):
            out[...] = ref[...]

    @pl.when(here > 0)
    def _():
        give_shares(first, chips, refs, highs, lows, w_ref, outs[0], outs[1:])


def keep_kernel(first, chips, att_ref, w_ref, *outs):
    att = att_ref[...]
    pieces = len(outs) // chips
    for i in range(chips):
        project(att, w_ref, first + i, 0, outs[i * pieces : (i + 1) * pieces])


def local_kernel(low_ref, high_ref, w_ref, *rest):
    att_ref, *gives = rest[-3:]
    rows = low_ref.shape[0]
    att_ref[:rows] = low_ref[...]
    att_ref[rows:] = high_ref[...]
    block = w_ref.shape[1] // lax.axis_size("head")
    cols = block // len(gives)
    for i, give_ref in enumerate(gives):
        start = pl.multiple_of(owner(0, 1) * block + i * cols, cols)
        give_ref[...] = jnp.dot(
            att_ref[...], w_ref[:, pl.ds(start, cols)], preferred_element_type=jnp.float32
        ).astype(jnp.bfloat16)


def sum_kernel(keep_ref, *rest):
    out_ref, at = rest[-1], 0
    for got in rest[:-1]:
        lanes = slice(at, at + got.shape[1])
        total = keep_ref[:, lanes].astype(jnp.float32) + got[...].astype(jnp.float32)
        out_ref[:, lanes] = total.astype(out_ref.dtype)
        at += got.shape[1]


def final_kernel(first, pieces, count, local_ref, *rest):
    out_hbm, held, sem = rest[-3:]
    rows, block = held.shape
    cols = block // pieces
    for i in range(pieces):
        here = slice(i * cols, (i + 1) * cols)
        total = local_ref[first : first + rows, here]
        for got in rest[i:count:pieces]:
            total = total + got[...].astype(jnp.float32)
        held[:, here] = total.astype(jnp.bfloat16)
    copy = pltpu.make_async_copy(held, out_hbm.at[pl.ds(first, rows)], sem)
    copy.start()
    copy.wait()


def body(queries, keys, values, segment_ids, out_weight):
    tokens, width = queries.shape
    kv_width = keys.shape[1]
    place_count = lax.axis_size("ctx")
    devices = lax.axis_size("head")
    chips = devices // CORES
    columns = out_weight.shape[1]
    block = columns // devices
    span = max(place_count // 16, 2)
    cut = int(tokens * CUT)
    bf16, f32 = jnp.bfloat16, jnp.float32
    dma = pltpu.SemaphoreType.DMA

    doc_row = segment_ids.reshape(1, tokens)
    groups = kv_width // HEAD_DIM
    packed_high = call(
        pack_kernel,
        pltpu.VMEM((2 * (tokens - cut) + DOC_ROWS, kv_width), bf16),
        [HBM] * 3,
        (far(keys), far(values), far(doc_row)),
        flops=2**33,
        scratch=[pltpu.VMEM((1, tokens), jnp.int32), dma((3,))],
    )
    packed_low, bias, column = call(
        mask_kernel,
        [
            pltpu.VMEM((2 * cut, kv_width), bf16),
            pltpu.VMEM((tokens, tokens), f32),
            pltpu.VMEM((tokens, tokens), f32),
        ],
        [VMEM] * 3,
        (keys, values, doc_row),
        flops=2**27,
    )
    highs, lows = [], []
    for s in range(1, span):
        ring = [(i, (i + s) % place_count) for i in range(place_count)]
        highs.append(lax.ppermute(packed_high, "ctx", ring))
        lows.append(lax.ppermute(packed_low, "ctx", ring[: place_count - s]))

    other_core = [(i, i ^ 1) for i in range(devices)]

    def keep_shares(att, first, count, pieces, flops):
        keep = pltpu.VMEM((att.shape[0], block // pieces), bf16)
        return call(
            functools.partial(keep_kernel, first, count),
            [keep] * (count * pieces),
            [VMEM] * 2,
            (near(att), out_weight),
            flops=flops,
        )

    def add(keep, dtype, *got):
        return call(
            sum_kernel,
            pltpu.VMEM(keep.shape, dtype),
            [VMEM] * (1 + len(got)),
            tuple(map(near, (keep, *got))),
        )

    def outputs(rows, pieces):
        share = pltpu.VMEM((rows, block // pieces), bf16)
        return [pltpu.VMEM((rows, width), bf16)] + [share] * ((chips - 1) * pieces)

    always = (queries, keys, values, near(bias), near(column), out_weight)
    done = call(
        functools.partial(first_kernel, cut, chips, 1 + (chips - 1) * PIECES),
        outputs(tokens - cut, PIECES) + outputs(cut, 1),
        [VMEM] * len(always),
        always,
        flops=2**27,
    )

    def shares(first, rows, pieces, keep_flops, lows, done, *after):
        prevs = highs + lows + done
        att, *gives = call(
            functools.partial(give_kernel, first, chips, len(done), len(highs), len(lows)),
            outputs(rows, pieces),
            [VMEM] * (len(always) + len(prevs)) + [ANY] * len(after),
            (*always, *map(near, prevs), *after),
            flops=8 * tokens * width * block,
        )
        keeps = keep_shares(att, 1, chips - 1, pieces, keep_flops)
        sums, arrived = [], []
        for i, (keep, give) in enumerate(zip(keeps, gives)):
            total = add(keep, bf16, lax.ppermute(give, "head", other_core))
            step = (i // pieces + 1) * CORES
            sums.append(total)
            arrived.append(
                lax.ppermute(total, "head", [(j, (j + step) % devices) for j in range(devices)])
            )
        return att, sums, arrived

    n_done = 1 + (chips - 1) * PIECES
    att_high, sums, high = shares(
        cut, tokens - cut, PIECES, 2**33, lows[:-1], list(done[:n_done])
    )
    att_low, sums, low = shares(0, cut, 1, 2**33, lows, list(done[n_done:]), *sums)

    att, *gives = call(
        local_kernel,
        [pltpu.VMEM((tokens, width), bf16)] + [pltpu.VMEM((tokens, block // 2), bf16)] * 2,
        [VMEM] * 3 + [ANY] * len(high),
        (near(att_low), near(att_high), out_weight, *high),
        flops=4 * tokens * width * block,
    )
    (keep,) = keep_shares(att, 0, 1, 1, 0)
    local = add(keep, f32, *[lax.ppermute(give, "head", other_core) for give in gives])

    def finish(first, rows, pieces, arrived, *out):
        return pl.pallas_call(
            functools.partial(final_kernel, first, pieces, len(arrived)),
            out_shape=pltpu.HBM((tokens, block), bf16),
            in_specs=[VMEM] * (1 + len(arrived)) + [HBM] * len(out),
            out_specs=HBM,
            scratch_shapes=[pltpu.VMEM((rows, block), bf16), dma],
            input_output_aliases={1 + len(arrived): 0} if out else {},
            cost_estimate=pl.CostEstimate(flops=0, bytes_accessed=0, transcendentals=0),
        )(near(local), *map(near, arrived), *out)

    return finish(0, cut, 1, low, finish(cut, tokens - cut, PIECES, high))


def solution(mesh):
    in_specs = (P("ctx", "head"), P("ctx", "head"), P("ctx", "head"), P("ctx"), P("head", None))
    out_specs = P("ctx", "head")
    return jax.shard_map(body, mesh=mesh, in_specs=in_specs, out_specs=out_specs, check_vma=False)
```

```python
import functools
import math

import jax
import jax.numpy as jnp
from jax import lax
from jax.experimental import pallas as pl
from jax.experimental.pallas import tpu as pltpu
from jax.sharding import PartitionSpec as P

HEAD_DIM = 128
CORES = 2
CUT = 160 / 256
DOC_ROWS = 16
PIECES = 1
LOW_PIECES = 2
LOG2_SCALE = math.log2(math.e) / math.sqrt(HEAD_DIM)
HIDDEN = -1e30
NT = (((1,), (1,)), ((), ()))
VMEM = pl.BlockSpec(memory_space=pltpu.VMEM)
ANY = pl.BlockSpec(memory_space=pl.ANY)
HBM = pl.BlockSpec(memory_space=pltpu.HBM)


def near(x):
    return pltpu.with_memory_space_constraint(x, pltpu.VMEM)


def far(x):
    return pltpu.with_memory_space_constraint(x, pltpu.HBM)


def call(kernel, out_shape, in_specs, args, flops=0, moved=0, vmem_mib=32, scratch=()):
    return pl.pallas_call(
        kernel,
        out_shape=out_shape,
        in_specs=in_specs,
        out_specs=jax.tree.map(lambda _: VMEM, out_shape),
        scratch_shapes=scratch,
        compiler_params=pltpu.CompilerParams(vmem_limit_bytes=vmem_mib * 2**20),
        cost_estimate=pl.CostEstimate(
            flops=flops, bytes_accessed=moved, transcendentals=0
        ),
    )(*args)


def pack_kernel(k_hbm, v_hbm, doc_hbm, high_ref, held, sem):
    tokens, width = k_hbm.shape
    rows = (high_ref.shape[0] - DOC_ROWS) // 2
    last = lax.axis_index("ctx") == lax.axis_size("ctx") - 1

    @pl.when(last)
    def _():
        high_ref[...] = jnp.zeros_like(high_ref)

    @pl.when(jnp.logical_not(last))
    def _():
        copies = [pltpu.make_async_copy(doc_hbm, held, sem.at[2])]
        for i, source in enumerate((k_hbm, v_hbm)):
            copies.append(
                pltpu.make_async_copy(
                    source.at[tokens - rows :], high_ref.at[i * rows : (i + 1) * rows], sem.at[i]
                )
            )
        for copy in copies:
            copy.start()
        copies[0].wait()
        docs = (held[...] + 1).astype(jnp.float32)
        parts = [docs[:, at : at + width] for at in range(0, tokens, width)]
        parts.append(jnp.zeros((DOC_ROWS - len(parts), width), jnp.float32))
        high_ref[2 * rows :, :] = jnp.concatenate(parts, axis=0).astype(jnp.bfloat16)
        for copy in copies[1:]:
            copy.wait()


def stacked(q_ref, r0, rows, first, repeats):
    heads = [
        q_ref[r0 : r0 + rows, h * HEAD_DIM : (h + 1) * HEAD_DIM]
        for h in range(first, first + repeats)
    ]
    return jnp.concatenate(heads, axis=0)


def with_ones(v):
    return jnp.concatenate([v, jnp.ones_like(v)], axis=1)


def hide(scores, bias):
    rows, count = bias.shape
    shape = (scores.shape[0] // rows, rows, count)
    return (scores.reshape(shape) + bias[None]).reshape(scores.shape)


def weights_of(scores, top):
    return jnp.exp2((scores - top) * LOG2_SCALE).astype(jnp.bfloat16)


def key_docs(high_ref, tokens):
    wide = high_ref[high_ref.shape[0] - DOC_ROWS :, :].astype(jnp.float32)
    parts = [wide[i : i + 1, :] for i in range(tokens // high_ref.shape[1])]
    return jnp.concatenate(parts, axis=1)


def attend(first, q_ref, bias_ref, column_ref, own_k, own_v, highs, lows, att_ref):
    tokens = q_ref.shape[0]
    rows = att_ref.shape[0]
    count = first + rows
    groups = own_k.shape[1] // HEAD_DIM
    repeats = q_ref.shape[1] // HEAD_DIM // groups
    column = column_ref[first:count, :]
    biases, keys, values = [], [], []
    for s, (high, low) in enumerate(zip(highs, lows), 1):
        n = (high.shape[0] - DOC_ROWS) // 2
        seen = tokens if low is not None else n
        if low is not None:
            keys.append(low[: tokens - n, :])
            values.append(low[tokens - n :, :])
        keys.append(high[:n, :])
        values.append(high[n : 2 * n, :])
        there = (lax.axis_index("ctx") >= s).astype(jnp.float32)
        same = key_docs(high, tokens)[:, tokens - seen :] * there == column[:, :seen]
        biases.append(jnp.where(same, 0.0, HIDDEN))
    place = 0 if first else len(biases)
    biases.insert(place, bias_ref[first:count, :count])
    keys.insert(place * 2, own_k[:count, :])
    values.insert(place * 2, own_v[:count, :])
    bias = jnp.concatenate(biases, axis=1)
    all_keys = jnp.concatenate(keys, axis=0)
    all_values = jnp.concatenate(values, axis=0)
    lanes = [slice(g * HEAD_DIM, (g + 1) * HEAD_DIM) for g in range(groups)]
    queries = [stacked(q_ref, first, rows, g * repeats, repeats) for g in range(groups)]
    scores = [
        lax.dot_general(q, all_keys[:, at], NT, preferred_element_type=jnp.float32)
        for q, at in zip(queries, lanes)
    ]
    scores = [hide(s, bias) for s in scores]
    tops = [jnp.max(s, axis=1, keepdims=True) for s in scores]
    weights = [weights_of(s, top) for s, top in zip(scores, tops)]
    summed = [
        jnp.dot(w, with_ones(all_values[:, at]), preferred_element_type=jnp.float32)
        for w, at in zip(weights, lanes)
    ]
    for g in range(groups):
        result = (summed[g][:, :HEAD_DIM] / summed[g][:, HEAD_DIM:]).astype(jnp.bfloat16)
        for r in range(repeats):
            h = g * repeats + r
            att_ref[:, h * HEAD_DIM : (h + 1) * HEAD_DIM] = result[r * rows : (r + 1) * rows]


def mask_kernel(k_ref, v_ref, doc_ref, low_ref, bias_ref, column_ref):
    tokens = doc_ref.shape[1]
    cut = low_ref.shape[0] // 2
    low_ref[:cut] = k_ref[:cut]
    low_ref[cut:] = v_ref[:cut]
    docs = jnp.broadcast_to(doc_ref[...].astype(jnp.float32) + 1.0, (tokens, tokens))
    columns = jnp.transpose(docs)
    at = lax.broadcasted_iota(jnp.int32, (tokens, tokens), 0)
    key = lax.broadcasted_iota(jnp.int32, (tokens, tokens), 1)
    bias_ref[...] = jnp.where((key <= at) & (docs == columns), 0.0, HIDDEN)
    column_ref[...] = columns


def owner(d, which):
    chips = lax.axis_size("head") // CORES
    me = lax.axis_index("head")
    chip, core = me // CORES, me % CORES
    return lax.rem(chip + d, chips) * CORES + lax.rem(core + which, CORES)


def project(att, w_ref, d, which, out_refs):
    block = w_ref.shape[1] // lax.axis_size("head")
    start = pl.multiple_of(owner(d, which) * block, block)
    share = jnp.dot(att, w_ref[:, pl.ds(start, block)], preferred_element_type=jnp.float32)
    cols = block // len(out_refs)
    for i, ref in enumerate(out_refs):
        ref[...] = share[:, i * cols : (i + 1) * cols].astype(jnp.bfloat16)


def give_shares(first, chips, refs, highs, lows, w_ref, att_ref, gives):
    attend(first, *refs, highs, lows, att_ref)
    att = att_ref[...]
    pieces = len(gives) // (chips - 1)
    for d in range(1, chips):
        project(att, w_ref, d, 1, gives[(d - 1) * pieces : d * pieces])


def first_kernel(cut, chips, n_outs, q_ref, k_ref, v_ref, bias_ref, column_ref, w_ref, *outs):
    refs = (q_ref, bias_ref, column_ref, k_ref, v_ref)
    highs, lows = outs[:n_outs], outs[n_outs:]

    @pl.when(lax.axis_index("ctx") == 0)
    def _():
        for first, (att_ref, *gives) in ((cut, highs), (0, lows)):
            give_shares(first, chips, refs, [], [], w_ref, att_ref, gives)


def give_kernel(
    first, chips, n_outs, n_high, n_low, q_ref, k_ref, v_ref, bias_ref, column_ref, w_ref, *rest
):
    outs = rest[-n_outs:]
    highs, lows = list(rest[:n_high]), list(rest[n_high : n_high + n_low])
    done = rest[n_high + n_low : n_high + n_low + n_outs]
    lows += [None] * (n_high - n_low)
    refs = (q_ref, bias_ref, column_ref, k_ref, v_ref)
    here = lax.axis_index("ctx")

    @pl.when(here == 0)
    def _():
        for ref, out in zip(done, outs):
            out[...] = ref[...]

    @pl.when(here > 0)
    def _():
        give_shares(first, chips, refs, highs, lows, w_ref, outs[0], outs[1:])


def keep_kernel(first, chips, att_ref, w_ref, *outs):
    att = att_ref[...]
    pieces = len(outs) // chips
    for i in range(chips):
        project(att, w_ref, first + i, 0, outs[i * pieces : (i + 1) * pieces])


def local_kernel(low_ref, high_ref, w_ref, *rest):
    att_ref, *gives = rest[-2:]
    rows = low_ref.shape[0]
    att_ref[:rows] = low_ref[...]
    att_ref[rows:] = high_ref[...]
    block = w_ref.shape[1] // lax.axis_size("head")
    cols = block // len(gives)
    for i, give_ref in enumerate(gives):
        start = pl.multiple_of(owner(0, 1) * block + i * cols, cols)
        give_ref[...] = jnp.dot(
            att_ref[...], w_ref[:, pl.ds(start, cols)], preferred_element_type=jnp.float32
        ).astype(jnp.bfloat16)


def sum_kernel(keep_ref, *rest):
    out_ref, at = rest[-1], 0
    for got in rest[:-1]:
        lanes = slice(at, at + got.shape[1])
        total = keep_ref[:, lanes].astype(jnp.float32) + got[...].astype(jnp.float32)
        out_ref[:, lanes] = total.astype(out_ref.dtype)
        at += got.shape[1]


def final_kernel(first, pieces, count, local_ref, *rest):
    out_hbm, held, sem = rest[-3:]
    rows, block = held.shape
    cols = block // pieces
    for i in range(pieces):
        here = slice(i * cols, (i + 1) * cols)
        total = local_ref[first : first + rows, here]
        for got in rest[i:count:pieces]:
            total = total + got[...].astype(jnp.float32)
        held[:, here] = total.astype(jnp.bfloat16)
    copy = pltpu.make_async_copy(held, out_hbm.at[pl.ds(first, rows)], sem)
    copy.start()
    copy.wait()


def body(queries, keys, values, segment_ids, out_weight):
    tokens, width = queries.shape
    kv_width = keys.shape[1]
    place_count = lax.axis_size("ctx")
    devices = lax.axis_size("head")
    chips = devices // CORES
    columns = out_weight.shape[1]
    block = columns // devices
    span = max(place_count // 16, 2)
    cut = int(tokens * CUT)
    bf16, f32 = jnp.bfloat16, jnp.float32
    dma = pltpu.SemaphoreType.DMA

    doc_row = segment_ids.reshape(1, tokens)
    groups = kv_width // HEAD_DIM
    packed_high = call(
        pack_kernel,
        pltpu.VMEM((2 * (tokens - cut) + DOC_ROWS, kv_width), bf16),
        [HBM] * 3,
        (far(keys), far(values), far(doc_row)),
        flops=2**33,
        scratch=[pltpu.VMEM((1, tokens), jnp.int32), dma((3,))],
    )
    packed_low, bias, column = call(
        mask_kernel,
        [
            pltpu.VMEM((2 * cut, kv_width), bf16),
            pltpu.VMEM((tokens, tokens), f32),
            pltpu.VMEM((tokens, tokens), f32),
        ],
        [VMEM] * 3,
        (keys, values, doc_row),
        flops=2**27,
    )
    highs, lows = [], []
    for s in range(1, span):
        ring = [(i, (i + s) % place_count) for i in range(place_count)]
        highs.append(lax.ppermute(packed_high, "ctx", ring))
        lows.append(lax.ppermute(packed_low, "ctx", ring[: place_count - s]))

    other_core = [(i, i ^ 1) for i in range(devices)]

    def keep_shares(att, first, count, pieces, flops):
        keep = pltpu.VMEM((att.shape[0], block // pieces), bf16)
        return call(
            functools.partial(keep_kernel, first, count),
            [keep] * (count * pieces),
            [VMEM] * 2,
            (near(att), out_weight),
            flops=flops,
        )

    def add(keep, dtype, *got):
        return call(
            sum_kernel,
            pltpu.VMEM(keep.shape, dtype),
            [VMEM] * (1 + len(got)),
            tuple(map(near, (keep, *got))),
        )

    def outputs(rows, pieces):
        share = pltpu.VMEM((rows, block // pieces), bf16)
        return [pltpu.VMEM((rows, width), bf16)] + [share] * ((chips - 1) * pieces)

    always = (queries, keys, values, near(bias), near(column), out_weight)
    done = call(
        functools.partial(first_kernel, cut, chips, 1 + (chips - 1) * PIECES),
        outputs(tokens - cut, PIECES) + outputs(cut, LOW_PIECES),
        [VMEM] * len(always),
        always,
        flops=2**27,
    )

    def shares(first, rows, pieces, keep_flops, lows, done, *after):
        prevs = highs + lows + done
        att, *gives = call(
            functools.partial(give_kernel, first, chips, len(done), len(highs), len(lows)),
            outputs(rows, pieces),
            [VMEM] * (len(always) + len(prevs)) + [ANY] * len(after),
            (*always, *map(near, prevs), *after),
            flops=8 * tokens * width * block,
        )
        keeps = keep_shares(att, 1, chips - 1, pieces, keep_flops)
        sums, arrived = [], []
        for i, (keep, give) in enumerate(zip(keeps, gives)):
            total = add(keep, bf16, lax.ppermute(give, "head", other_core))
            step = (i // pieces + 1) * CORES
            sums.append(total)
            arrived.append(
                lax.ppermute(total, "head", [(j, (j + step) % devices) for j in range(devices)])
            )
        return att, sums, arrived

    n_done = 1 + (chips - 1) * PIECES
    att_high, sums, high = shares(
        cut, tokens - cut, PIECES, 2**33, lows[:-1], list(done[:n_done])
    )
    att_low, sums, low = shares(0, cut, LOW_PIECES, 2**33, lows, list(done[n_done:]), *sums)

    att, *gives = call(
        local_kernel,
        [pltpu.VMEM((tokens, width), bf16)] + [pltpu.VMEM((tokens, block), bf16)],
        [VMEM] * 3 + [ANY] * len(high),
        (near(att_low), near(att_high), out_weight, *high),
        flops=4 * tokens * width * block,
    )
    (keep,) = keep_shares(att, 0, 1, 1, 2**33)
    local = add(keep, f32, *[lax.ppermute(give, "head", other_core) for give in gives])

    def finish(first, rows, pieces, arrived, *out):
        return pl.pallas_call(
            functools.partial(final_kernel, first, pieces, len(arrived)),
            out_shape=pltpu.HBM((tokens, block), bf16),
            in_specs=[VMEM] * (1 + len(arrived)) + [HBM] * len(out),
            out_specs=HBM,
            scratch_shapes=[pltpu.VMEM((rows, block), bf16), dma],
            input_output_aliases={1 + len(arrived): 0} if out else {},
            cost_estimate=pl.CostEstimate(flops=0, bytes_accessed=0, transcendentals=0),
        )(near(local), *map(near, arrived), *out)

    return finish(0, cut, LOW_PIECES, low, finish(cut, tokens - cut, PIECES, high))


def solution(mesh):
    in_specs = (P("ctx", "head"), P("ctx", "head"), P("ctx", "head"), P("ctx"), P("head", None))
    out_specs = P("ctx", "head")
    return jax.shard_map(body, mesh=mesh, in_specs=in_specs, out_specs=out_specs, check_vma=False)
```

```python
import functools
import math

import jax
import jax.numpy as jnp
from jax import lax
from jax.experimental import pallas as pl
from jax.experimental.pallas import tpu as pltpu
from jax.sharding import PartitionSpec as P

HEAD_DIM = 128
CORES = 2
CUT = 160 / 256
DOC_ROWS = 16
PIECES = 1
LOW_PIECES = 2
LOG2_SCALE = math.log2(math.e) / math.sqrt(HEAD_DIM)
HIDDEN = -1e30
NT = (((1,), (1,)), ((), ()))
VMEM = pl.BlockSpec(memory_space=pltpu.VMEM)
ANY = pl.BlockSpec(memory_space=pl.ANY)
HBM = pl.BlockSpec(memory_space=pltpu.HBM)


def near(x):
    return pltpu.with_memory_space_constraint(x, pltpu.VMEM)


def far(x):
    return pltpu.with_memory_space_constraint(x, pltpu.HBM)


def call(kernel, out_shape, in_specs, args, flops=0, moved=0, vmem_mib=32, scratch=()):
    return pl.pallas_call(
        kernel,
        out_shape=out_shape,
        in_specs=in_specs,
        out_specs=jax.tree.map(lambda _: VMEM, out_shape),
        scratch_shapes=scratch,
        compiler_params=pltpu.CompilerParams(vmem_limit_bytes=vmem_mib * 2**20),
        cost_estimate=pl.CostEstimate(
            flops=flops, bytes_accessed=moved, transcendentals=0
        ),
    )(*args)


def pack_kernel(k_hbm, v_hbm, doc_hbm, high_ref, held, sem):
    tokens, width = k_hbm.shape
    rows = (high_ref.shape[0] - DOC_ROWS) // 2
    last = lax.axis_index("ctx") == lax.axis_size("ctx") - 1

    @pl.when(last)
    def _():
        high_ref[...] = jnp.zeros_like(high_ref)

    @pl.when(jnp.logical_not(last))
    def _():
        copies = [pltpu.make_async_copy(doc_hbm, held, sem.at[2])]
        for i, source in enumerate((k_hbm, v_hbm)):
            copies.append(
                pltpu.make_async_copy(
                    source.at[tokens - rows :], high_ref.at[i * rows : (i + 1) * rows], sem.at[i]
                )
            )
        for copy in copies:
            copy.start()
        copies[0].wait()
        docs = (held[...] + 1).astype(jnp.float32)
        parts = [docs[:, at : at + width] for at in range(0, tokens, width)]
        parts.append(jnp.zeros((DOC_ROWS - len(parts), width), jnp.float32))
        high_ref[2 * rows :, :] = jnp.concatenate(parts, axis=0).astype(jnp.bfloat16)
        for copy in copies[1:]:
            copy.wait()


def stacked(q_ref, r0, rows, first, repeats):
    heads = [
        q_ref[r0 : r0 + rows, h * HEAD_DIM : (h + 1) * HEAD_DIM]
        for h in range(first, first + repeats)
    ]
    return jnp.concatenate(heads, axis=0)


def with_ones(v):
    return jnp.concatenate([v, jnp.ones_like(v)], axis=1)


def hide(scores, bias):
    rows, count = bias.shape
    shape = (scores.shape[0] // rows, rows, count)
    return (scores.reshape(shape) + bias[None]).reshape(scores.shape)


def weights_of(scores, top):
    return jnp.exp2((scores - top) * LOG2_SCALE).astype(jnp.bfloat16)


def key_docs(high_ref, tokens):
    wide = high_ref[high_ref.shape[0] - DOC_ROWS :, :].astype(jnp.float32)
    parts = [wide[i : i + 1, :] for i in range(tokens // high_ref.shape[1])]
    return jnp.concatenate(parts, axis=1)


def attend(first, q_ref, bias_ref, column_ref, own_k, own_v, highs, lows, att_ref):
    tokens = q_ref.shape[0]
    rows = att_ref.shape[0]
    count = first + rows
    groups = own_k.shape[1] // HEAD_DIM
    repeats = q_ref.shape[1] // HEAD_DIM // groups
    column = column_ref[first:count, :]
    biases, keys, values = [], [], []
    for s, (high, low) in enumerate(zip(highs, lows), 1):
        n = (high.shape[0] - DOC_ROWS) // 2
        seen = tokens if low is not None else n
        if low is not None:
            keys.append(low[: tokens - n, :])
            values.append(low[tokens - n :, :])
        keys.append(high[:n, :])
        values.append(high[n : 2 * n, :])
        there = (lax.axis_index("ctx") >= s).astype(jnp.float32)
        same = key_docs(high, tokens)[:, tokens - seen :] * there == column[:, :seen]
        biases.append(jnp.where(same, 0.0, HIDDEN))
    place = 0 if first else len(biases)
    biases.insert(place, bias_ref[first:count, :count])
    keys.insert(place * 2, own_k[:count, :])
    values.insert(place * 2, own_v[:count, :])
    bias = jnp.concatenate(biases, axis=1)
    all_keys = jnp.concatenate(keys, axis=0)
    all_values = jnp.concatenate(values, axis=0)
    lanes = [slice(g * HEAD_DIM, (g + 1) * HEAD_DIM) for g in range(groups)]
    queries = [stacked(q_ref, first, rows, g * repeats, repeats) for g in range(groups)]
    scores = [
        lax.dot_general(q, all_keys[:, at], NT, preferred_element_type=jnp.float32)
        for q, at in zip(queries, lanes)
    ]
    scores = [hide(s, bias) for s in scores]
    tops = [jnp.max(s, axis=1, keepdims=True) for s in scores]
    weights = [weights_of(s, top) for s, top in zip(scores, tops)]
    summed = [
        jnp.dot(w, with_ones(all_values[:, at]), preferred_element_type=jnp.float32)
        for w, at in zip(weights, lanes)
    ]
    for g in range(groups):
        result = (summed[g][:, :HEAD_DIM] / summed[g][:, HEAD_DIM:]).astype(jnp.bfloat16)
        for r in range(repeats):
            h = g * repeats + r
            att_ref[:, h * HEAD_DIM : (h + 1) * HEAD_DIM] = result[r * rows : (r + 1) * rows]


def mask_kernel(k_ref, v_ref, doc_ref, low_ref, bias_ref, column_ref):
    tokens = doc_ref.shape[1]
    cut = low_ref.shape[0] // 2
    low_ref[:cut] = k_ref[:cut]
    low_ref[cut:] = v_ref[:cut]
    docs = jnp.broadcast_to(doc_ref[...].astype(jnp.float32) + 1.0, (tokens, tokens))
    columns = jnp.transpose(docs)
    at = lax.broadcasted_iota(jnp.int32, (tokens, tokens), 0)
    key = lax.broadcasted_iota(jnp.int32, (tokens, tokens), 1)
    bias_ref[...] = jnp.where((key <= at) & (docs == columns), 0.0, HIDDEN)
    column_ref[...] = columns


def owner(d, which):
    chips = lax.axis_size("head") // CORES
    me = lax.axis_index("head")
    chip, core = me // CORES, me % CORES
    return lax.rem(chip + d, chips) * CORES + lax.rem(core + which, CORES)


def project(att, w_ref, d, which, out_refs):
    block = w_ref.shape[1] // lax.axis_size("head")
    start = pl.multiple_of(owner(d, which) * block, block)
    share = jnp.dot(att, w_ref[:, pl.ds(start, block)], preferred_element_type=jnp.float32)
    cols = block // len(out_refs)
    for i, ref in enumerate(out_refs):
        ref[...] = share[:, i * cols : (i + 1) * cols].astype(jnp.bfloat16)


def give_shares(first, chips, refs, highs, lows, w_ref, att_ref, gives):
    attend(first, *refs, highs, lows, att_ref)
    att = att_ref[...]
    pieces = len(gives) // (chips - 1)
    for d in range(1, chips):
        project(att, w_ref, d, 1, gives[(d - 1) * pieces : d * pieces])


def first_kernel(cut, chips, n_outs, q_ref, k_ref, v_ref, bias_ref, column_ref, w_ref, *outs):
    refs = (q_ref, bias_ref, column_ref, k_ref, v_ref)
    highs, lows = outs[:n_outs], outs[n_outs:]

    @pl.when(lax.axis_index("ctx") == 0)
    def _():
        for first, (att_ref, *gives) in ((cut, highs), (0, lows)):
            give_shares(first, chips, refs, [], [], w_ref, att_ref, gives)


def give_kernel(
    first, chips, n_outs, n_high, n_low, q_ref, k_ref, v_ref, bias_ref, column_ref, w_ref, *rest
):
    outs = rest[-n_outs:]
    highs, lows = list(rest[:n_high]), list(rest[n_high : n_high + n_low])
    done = rest[n_high + n_low : n_high + n_low + n_outs]
    lows += [None] * (n_high - n_low)
    refs = (q_ref, bias_ref, column_ref, k_ref, v_ref)
    here = lax.axis_index("ctx")

    @pl.when(here == 0)
    def _():
        for ref, out in zip(done, outs):
            out[...] = ref[...]

    @pl.when(here > 0)
    def _():
        give_shares(first, chips, refs, highs, lows, w_ref, outs[0], outs[1:])


def keep_kernel(first, chips, att_ref, w_ref, *outs):
    att = att_ref[...]
    pieces = len(outs) // chips
    for i in range(chips):
        project(att, w_ref, first + i, 0, outs[i * pieces : (i + 1) * pieces])


def local_kernel(low_ref, high_ref, w_ref, *rest):
    att_ref, *gives = rest[-2:]
    rows = low_ref.shape[0]
    att_ref[:rows] = low_ref[...]
    att_ref[rows:] = high_ref[...]
    block = w_ref.shape[1] // lax.axis_size("head")
    cols = block // len(gives)
    for i, give_ref in enumerate(gives):
        start = pl.multiple_of(owner(0, 1) * block + i * cols, cols)
        give_ref[...] = jnp.dot(
            att_ref[...], w_ref[:, pl.ds(start, cols)], preferred_element_type=jnp.float32
        ).astype(jnp.bfloat16)


def sum_kernel(count, keep_ref, *rest):
    out_ref, at = rest[-1], 0
    for got in rest[:count]:
        lanes = slice(at, at + got.shape[1])
        total = keep_ref[:, lanes].astype(jnp.float32) + got[...].astype(jnp.float32)
        out_ref[:, lanes] = total.astype(out_ref.dtype)
        at += got.shape[1]


def final_kernel(first, pieces, count, local_ref, *rest):
    out_hbm, held, sem = rest[-3:]
    rows, block = held.shape
    cols = block // pieces
    for i in range(pieces):
        here = slice(i * cols, (i + 1) * cols)
        total = local_ref[first : first + rows, here]
        for got in rest[i:count:pieces]:
            total = total + got[...].astype(jnp.float32)
        held[:, here] = total.astype(jnp.bfloat16)
    copy = pltpu.make_async_copy(held, out_hbm.at[pl.ds(first, rows)], sem)
    copy.start()
    copy.wait()


def body(queries, keys, values, segment_ids, out_weight):
    tokens, width = queries.shape
    kv_width = keys.shape[1]
    place_count = lax.axis_size("ctx")
    devices = lax.axis_size("head")
    chips = devices // CORES
    columns = out_weight.shape[1]
    block = columns // devices
    span = max(place_count // 16, 2)
    cut = int(tokens * CUT)
    bf16, f32 = jnp.bfloat16, jnp.float32
    dma = pltpu.SemaphoreType.DMA

    doc_row = segment_ids.reshape(1, tokens)
    groups = kv_width // HEAD_DIM
    packed_high = call(
        pack_kernel,
        pltpu.VMEM((2 * (tokens - cut) + DOC_ROWS, kv_width), bf16),
        [HBM] * 3,
        (far(keys), far(values), far(doc_row)),
        flops=2**33,
        scratch=[pltpu.VMEM((1, tokens), jnp.int32), dma((3,))],
    )
    packed_low, bias, column = call(
        mask_kernel,
        [
            pltpu.VMEM((2 * cut, kv_width), bf16),
            pltpu.VMEM((tokens, tokens), f32),
            pltpu.VMEM((tokens, tokens), f32),
        ],
        [VMEM] * 3,
        (keys, values, doc_row),
        flops=2**27,
    )
    highs, lows = [], []
    for s in range(1, span):
        ring = [(i, (i + s) % place_count) for i in range(place_count)]
        highs.append(lax.ppermute(packed_high, "ctx", ring))
        lows.append(lax.ppermute(packed_low, "ctx", ring[: place_count - s]))

    other_core = [(i, i ^ 1) for i in range(devices)]

    def keep_shares(att, first, count, pieces, flops):
        keep = pltpu.VMEM((att.shape[0], block // pieces), bf16)
        return call(
            functools.partial(keep_kernel, first, count),
            [keep] * (count * pieces),
            [VMEM] * 2,
            (near(att), out_weight),
            flops=flops,
        )

    def add(keep, dtype, *got, after=()):
        return call(
            functools.partial(sum_kernel, len(got)),
            pltpu.VMEM(keep.shape, dtype),
            [VMEM] * (1 + len(got)) + [ANY] * len(after),
            (*map(near, (keep, *got)), *after),
        )

    def outputs(rows, pieces):
        share = pltpu.VMEM((rows, block // pieces), bf16)
        return [pltpu.VMEM((rows, width), bf16)] + [share] * ((chips - 1) * pieces)

    always = (queries, keys, values, near(bias), near(column), out_weight)
    done = call(
        functools.partial(first_kernel, cut, chips, 1 + (chips - 1) * PIECES),
        outputs(tokens - cut, PIECES) + outputs(cut, LOW_PIECES),
        [VMEM] * len(always),
        always,
        flops=2**27,
    )

    def shares(first, rows, pieces, keep_flops, lows, done, *after):
        prevs = highs + lows + done
        att, *gives = call(
            functools.partial(give_kernel, first, chips, len(done), len(highs), len(lows)),
            outputs(rows, pieces),
            [VMEM] * (len(always) + len(prevs)) + [ANY] * len(after),
            (*always, *map(near, prevs), *after),
            flops=8 * tokens * width * block,
        )
        keeps = keep_shares(att, 1, chips - 1, pieces, keep_flops)
        sums, arrived = [], []
        for i, (keep, give) in enumerate(zip(keeps, gives)):
            total = add(keep, bf16, lax.ppermute(give, "head", other_core), after=sums[-1:])
            step = (i // pieces + 1) * CORES
            sums.append(total)
            arrived.append(
                lax.ppermute(total, "head", [(j, (j + step) % devices) for j in range(devices)])
            )
        return att, sums, arrived

    n_done = 1 + (chips - 1) * PIECES
    att_high, sums, high = shares(
        cut, tokens - cut, PIECES, 2**33, lows[:-1], list(done[:n_done])
    )
    att_low, sums, low = shares(0, cut, LOW_PIECES, 2**33, lows, list(done[n_done:]), *sums)

    att, *gives = call(
        local_kernel,
        [pltpu.VMEM((tokens, width), bf16)] + [pltpu.VMEM((tokens, block), bf16)],
        [VMEM] * 3 + [ANY] * len(high),
        (near(att_low), near(att_high), out_weight, *high),
        flops=4 * tokens * width * block,
    )
    (keep,) = keep_shares(att, 0, 1, 1, 2**33)
    local = add(keep, f32, *[lax.ppermute(give, "head", other_core) for give in gives])

    def finish(first, rows, pieces, arrived, *out):
        return pl.pallas_call(
            functools.partial(final_kernel, first, pieces, len(arrived)),
            out_shape=pltpu.HBM((tokens, block), bf16),
            in_specs=[VMEM] * (1 + len(arrived)) + [HBM] * len(out),
            out_specs=HBM,
            scratch_shapes=[pltpu.VMEM((rows, block), bf16), dma],
            input_output_aliases={1 + len(arrived): 0} if out else {},
            cost_estimate=pl.CostEstimate(flops=0, bytes_accessed=0, transcendentals=0),
        )(near(local), *map(near, arrived), *out)

    return finish(0, cut, LOW_PIECES, low, finish(cut, tokens - cut, PIECES, high))


def solution(mesh):
    in_specs = (P("ctx", "head"), P("ctx", "head"), P("ctx", "head"), P("ctx"), P("head", None))
    out_specs = P("ctx", "head")
    return jax.shard_map(body, mesh=mesh, in_specs=in_specs, out_specs=out_specs, check_vma=False)
```

```python
import functools
import math

import jax
import jax.numpy as jnp
from jax import lax
from jax.experimental import pallas as pl
from jax.experimental.pallas import tpu as pltpu
from jax.sharding import PartitionSpec as P

HEAD_DIM = 128
CORES = 2
CUT = 160 / 256
DOC_ROWS = 16
PIECES = 1
LOG2_SCALE = math.log2(math.e) / math.sqrt(HEAD_DIM)
HIDDEN = -1e30
NT = (((1,), (1,)), ((), ()))
VMEM = pl.BlockSpec(memory_space=pltpu.VMEM)
ANY = pl.BlockSpec(memory_space=pl.ANY)
HBM = pl.BlockSpec(memory_space=pltpu.HBM)


def near(x):
    return pltpu.with_memory_space_constraint(x, pltpu.VMEM)


def far(x):
    return pltpu.with_memory_space_constraint(x, pltpu.HBM)


def call(kernel, out_shape, in_specs, args, flops=0, moved=0, vmem_mib=32, scratch=()):
    return pl.pallas_call(
        kernel,
        out_shape=out_shape,
        in_specs=in_specs,
        out_specs=jax.tree.map(lambda _: VMEM, out_shape),
        scratch_shapes=scratch,
        compiler_params=pltpu.CompilerParams(vmem_limit_bytes=vmem_mib * 2**20),
        cost_estimate=pl.CostEstimate(
            flops=flops, bytes_accessed=moved, transcendentals=0
        ),
    )(*args)


def pack_kernel(k_hbm, v_hbm, doc_hbm, high_ref, held, sem):
    tokens, width = k_hbm.shape
    rows = (high_ref.shape[0] - DOC_ROWS) // 2
    last = lax.axis_index("ctx") == lax.axis_size("ctx") - 1

    @pl.when(last)
    def _():
        high_ref[...] = jnp.zeros_like(high_ref)

    @pl.when(jnp.logical_not(last))
    def _():
        copies = [pltpu.make_async_copy(doc_hbm, held, sem.at[2])]
        for i, source in enumerate((k_hbm, v_hbm)):
            copies.append(
                pltpu.make_async_copy(
                    source.at[tokens - rows :], high_ref.at[i * rows : (i + 1) * rows], sem.at[i]
                )
            )
        for copy in copies:
            copy.start()
        copies[0].wait()
        docs = (held[...] + 1).astype(jnp.float32)
        parts = [docs[:, at : at + width] for at in range(0, tokens, width)]
        parts.append(jnp.zeros((DOC_ROWS - len(parts), width), jnp.float32))
        high_ref[2 * rows :, :] = jnp.concatenate(parts, axis=0).astype(jnp.bfloat16)
        for copy in copies[1:]:
            copy.wait()


def stacked(q_ref, r0, rows, first, repeats):
    heads = [
        q_ref[r0 : r0 + rows, h * HEAD_DIM : (h + 1) * HEAD_DIM]
        for h in range(first, first + repeats)
    ]
    return jnp.concatenate(heads, axis=0)


def with_ones(v):
    return jnp.concatenate([v, jnp.ones_like(v)], axis=1)


def hide(scores, bias):
    rows, count = bias.shape
    shape = (scores.shape[0] // rows, rows, count)
    return (scores.reshape(shape) + bias[None]).reshape(scores.shape)


def weights_of(scores, top):
    return jnp.exp2((scores - top) * LOG2_SCALE).astype(jnp.bfloat16)


def key_docs(high_ref, tokens):
    wide = high_ref[high_ref.shape[0] - DOC_ROWS :, :].astype(jnp.float32)
    parts = [wide[i : i + 1, :] for i in range(tokens // high_ref.shape[1])]
    return jnp.concatenate(parts, axis=1)


def attend(first, q_ref, bias_ref, column_ref, own_k, own_v, highs, lows, att_ref):
    tokens = q_ref.shape[0]
    rows = att_ref.shape[0]
    count = first + rows
    groups = own_k.shape[1] // HEAD_DIM
    repeats = q_ref.shape[1] // HEAD_DIM // groups
    column = column_ref[first:count, :]
    biases, keys, values = [], [], []
    for s, (high, low) in enumerate(zip(highs, lows), 1):
        n = (high.shape[0] - DOC_ROWS) // 2
        seen = tokens if low is not None else n
        if low is not None:
            keys.append(low[: tokens - n, :])
            values.append(low[tokens - n :, :])
        keys.append(high[:n, :])
        values.append(high[n : 2 * n, :])
        there = (lax.axis_index("ctx") >= s).astype(jnp.float32)
        same = key_docs(high, tokens)[:, tokens - seen :] * there == column[:, :seen]
        biases.append(jnp.where(same, 0.0, HIDDEN))
    place = 0 if first else len(biases)
    biases.insert(place, bias_ref[first:count, :count])
    keys.insert(place * 2, own_k[:count, :])
    values.insert(place * 2, own_v[:count, :])
    bias = jnp.concatenate(biases, axis=1)
    all_keys = jnp.concatenate(keys, axis=0)
    all_values = jnp.concatenate(values, axis=0)
    lanes = [slice(g * HEAD_DIM, (g + 1) * HEAD_DIM) for g in range(groups)]
    queries = [stacked(q_ref, first, rows, g * repeats, repeats) for g in range(groups)]
    scores = [
        lax.dot_general(q, all_keys[:, at], NT, preferred_element_type=jnp.float32)
        for q, at in zip(queries, lanes)
    ]
    scores = [hide(s, bias) for s in scores]
    tops = [jnp.max(s, axis=1, keepdims=True) for s in scores]
    weights = [weights_of(s, top) for s, top in zip(scores, tops)]
    summed = [
        jnp.dot(w, with_ones(all_values[:, at]), preferred_element_type=jnp.float32)
        for w, at in zip(weights, lanes)
    ]
    for g in range(groups):
        result = (summed[g][:, :HEAD_DIM] / summed[g][:, HEAD_DIM:]).astype(jnp.bfloat16)
        for r in range(repeats):
            h = g * repeats + r
            att_ref[:, h * HEAD_DIM : (h + 1) * HEAD_DIM] = result[r * rows : (r + 1) * rows]


def mask_kernel(k_ref, v_ref, doc_ref, low_ref, bias_ref, column_ref):
    tokens = doc_ref.shape[1]
    cut = low_ref.shape[0] // 2
    low_ref[:cut] = k_ref[:cut]
    low_ref[cut:] = v_ref[:cut]
    docs = jnp.broadcast_to(doc_ref[...].astype(jnp.float32) + 1.0, (tokens, tokens))
    columns = jnp.transpose(docs)
    at = lax.broadcasted_iota(jnp.int32, (tokens, tokens), 0)
    key = lax.broadcasted_iota(jnp.int32, (tokens, tokens), 1)
    bias_ref[...] = jnp.where((key <= at) & (docs == columns), 0.0, HIDDEN)
    column_ref[...] = columns


def own_kernel(q_ref, k_ref, v_ref, bias_ref, acc_ref, total_ref, top_ref):
    groups = k_ref.shape[1] // HEAD_DIM
    repeats = q_ref.shape[1] // HEAD_DIM // groups
    rows = acc_ref.shape[1] // repeats

    @pl.when(lax.axis_index("ctx") > 0)
    def _():
        lanes = [slice(g * HEAD_DIM, (g + 1) * HEAD_DIM) for g in range(groups)]
        scores = [
            lax.dot_general(
                stacked(q_ref, 0, rows, g * repeats, repeats),
                k_ref[:rows, lanes[g]],
                NT,
                preferred_element_type=jnp.float32,
            )
            for g in range(groups)
        ]
        scores = [hide(s, bias_ref[:rows, :rows]) for s in scores]
        tops = [jnp.max(s, axis=1, keepdims=True) for s in scores]
        weights = [weights_of(s, top) for s, top in zip(scores, tops)]
        for g in range(groups):
            summed = jnp.dot(
                weights[g], with_ones(v_ref[:rows, lanes[g]]), preferred_element_type=jnp.float32
            )
            acc_ref[g] = summed[:, :HEAD_DIM]
            total_ref[g] = summed[:, HEAD_DIM:]
            top_ref[g] = jnp.broadcast_to(tops[g], acc_ref.shape[1:])


def attend_before(q_ref, column_ref, state, highs, lows, att_ref):
    acc_ref, total_ref, top_ref = state
    tokens, width = q_ref.shape
    rows = att_ref.shape[0]
    groups = acc_ref.shape[0]
    repeats = width // HEAD_DIM // groups
    column = column_ref[:rows, :]
    biases, keys, values = [], [], []
    for s, (high, low) in enumerate(zip(highs, lows), 1):
        keys += [low[:rows, :], high[: tokens - rows, :]]
        values += [low[rows:, :], high[tokens - rows : 2 * (tokens - rows), :]]
        there = (lax.axis_index("ctx") >= s).astype(jnp.float32)
        same = key_docs(high, tokens) * there == column
        biases.append(jnp.where(same, 0.0, HIDDEN))
    bias = jnp.concatenate(biases, axis=1)
    all_keys = jnp.concatenate(keys, axis=0)
    all_values = jnp.concatenate(values, axis=0)
    spread = bias.shape[1] // HEAD_DIM
    lanes = [slice(g * HEAD_DIM, (g + 1) * HEAD_DIM) for g in range(groups)]
    scores = [
        lax.dot_general(
            stacked(q_ref, 0, rows, g * repeats, repeats),
            all_keys[:, lanes[g]],
            NT,
            preferred_element_type=jnp.float32,
        )
        for g in range(groups)
    ]
    scores = [hide(x, bias) for x in scores]
    tops = [
        jnp.maximum(top_ref[g], jnp.max(scores[g], axis=1, keepdims=True)) for g in range(groups)
    ]
    weights = [
        weights_of(x, jnp.concatenate([top] * spread, axis=1)) for x, top in zip(scores, tops)
    ]
    for g in range(groups):
        factor = jnp.exp2((top_ref[g] - tops[g]) * LOG2_SCALE)
        summed = jnp.dot(
            weights[g], with_ones(all_values[:, lanes[g]]), preferred_element_type=jnp.float32
        )
        acc = acc_ref[g] * factor + summed[:, :HEAD_DIM]
        total = total_ref[g] * factor + summed[:, HEAD_DIM:]
        result = (acc / total).astype(jnp.bfloat16)
        for r in range(repeats):
            h = g * repeats + r
            att_ref[:, h * HEAD_DIM : (h + 1) * HEAD_DIM] = result[r * rows : (r + 1) * rows]


def owner(d, which):
    chips = lax.axis_size("head") // CORES
    me = lax.axis_index("head")
    chip, core = me // CORES, me % CORES
    return lax.rem(chip + d, chips) * CORES + lax.rem(core + which, CORES)


def project(att, w_ref, d, which, out_refs):
    block = w_ref.shape[1] // lax.axis_size("head")
    start = pl.multiple_of(owner(d, which) * block, block)
    share = jnp.dot(att, w_ref[:, pl.ds(start, block)], preferred_element_type=jnp.float32)
    cols = block // len(out_refs)
    for i, ref in enumerate(out_refs):
        ref[...] = share[:, i * cols : (i + 1) * cols].astype(jnp.bfloat16)


def give_shares(first, chips, refs, highs, lows, w_ref, att_ref, gives):
    attend(first, *refs, highs, lows, att_ref)
    att = att_ref[...]
    pieces = len(gives) // (chips - 1)
    for d in range(1, chips):
        project(att, w_ref, d, 1, gives[(d - 1) * pieces : d * pieces])


def first_kernel(cut, chips, n_outs, q_ref, k_ref, v_ref, bias_ref, column_ref, w_ref, *outs):
    refs = (q_ref, bias_ref, column_ref, k_ref, v_ref)
    highs, lows = outs[:n_outs], outs[n_outs:]

    @pl.when(lax.axis_index("ctx") == 0)
    def _():
        for first, (att_ref, *gives) in ((cut, highs), (0, lows)):
            give_shares(first, chips, refs, [], [], w_ref, att_ref, gives)


def give_kernel(
    first, chips, n_outs, n_high, n_low, q_ref, k_ref, v_ref, bias_ref, column_ref, w_ref, *rest
):
    outs = rest[-n_outs:]
    highs, lows = list(rest[:n_high]), list(rest[n_high : n_high + n_low])
    done = rest[n_high + n_low : n_high + n_low + n_outs]
    lows += [None] * (n_high - n_low)
    refs = (q_ref, bias_ref, column_ref, k_ref, v_ref)
    here = lax.axis_index("ctx")

    @pl.when(here == 0)
    def _():
        for ref, out in zip(done, outs):
            out[...] = ref[...]

    @pl.when(here > 0)
    def _():
        give_shares(first, chips, refs, highs, lows, w_ref, outs[0], outs[1:])


def low_kernel(
    chips, n_outs, n_prev, q_ref, column_ref, acc_ref, total_ref, top_ref, w_ref, *rest
):
    outs = rest[-n_outs:]
    highs, lows = rest[:n_prev], rest[n_prev : 2 * n_prev]
    done = rest[2 * n_prev : 2 * n_prev + n_outs]
    here = lax.axis_index("ctx")

    @pl.when(here == 0)
    def _():
        for ref, out in zip(done, outs):
            out[...] = ref[...]

    @pl.when(here > 0)
    def _():
        att_ref, gives = outs[0], outs[1:]
        attend_before(q_ref, column_ref, (acc_ref, total_ref, top_ref), highs, lows, att_ref)
        att = att_ref[...]
        for d in range(1, chips):
            project(att, w_ref, d, 1, gives[d - 1 : d])


def keep_kernel(first, chips, att_ref, w_ref, *outs):
    att = att_ref[...]
    pieces = len(outs) // chips
    for i in range(chips):
        project(att, w_ref, first + i, 0, outs[i * pieces : (i + 1) * pieces])


def local_kernel(low_ref, high_ref, w_ref, *rest):
    att_ref, *gives = rest[-3:]
    rows = low_ref.shape[0]
    att_ref[:rows] = low_ref[...]
    att_ref[rows:] = high_ref[...]
    block = w_ref.shape[1] // lax.axis_size("head")
    cols = block // len(gives)
    for i, give_ref in enumerate(gives):
        start = pl.multiple_of(owner(0, 1) * block + i * cols, cols)
        give_ref[...] = jnp.dot(
            att_ref[...], w_ref[:, pl.ds(start, cols)], preferred_element_type=jnp.float32
        ).astype(jnp.bfloat16)


def sum_kernel(keep_ref, *rest):
    out_ref, at = rest[-1], 0
    for got in rest[:-1]:
        lanes = slice(at, at + got.shape[1])
        total = keep_ref[:, lanes].astype(jnp.float32) + got[...].astype(jnp.float32)
        out_ref[:, lanes] = total.astype(out_ref.dtype)
        at += got.shape[1]


def final_kernel(first, pieces, count, local_ref, *rest):
    out_hbm, held, sem = rest[-3:]
    rows, block = held.shape
    cols = block // pieces
    for i in range(pieces):
        here = slice(i * cols, (i + 1) * cols)
        total = local_ref[first : first + rows, here]
        for got in rest[i:count:pieces]:
            total = total + got[...].astype(jnp.float32)
        held[:, here] = total.astype(jnp.bfloat16)
    copy = pltpu.make_async_copy(held, out_hbm.at[pl.ds(first, rows)], sem)
    copy.start()
    copy.wait()


def body(queries, keys, values, segment_ids, out_weight):
    tokens, width = queries.shape
    kv_width = keys.shape[1]
    place_count = lax.axis_size("ctx")
    devices = lax.axis_size("head")
    chips = devices // CORES
    columns = out_weight.shape[1]
    block = columns // devices
    span = max(place_count // 16, 2)
    cut = int(tokens * CUT)
    bf16, f32 = jnp.bfloat16, jnp.float32
    dma = pltpu.SemaphoreType.DMA

    doc_row = segment_ids.reshape(1, tokens)
    groups = kv_width // HEAD_DIM
    packed_high = call(
        pack_kernel,
        pltpu.VMEM((2 * (tokens - cut) + DOC_ROWS, kv_width), bf16),
        [HBM] * 3,
        (far(keys), far(values), far(doc_row)),
        flops=2**33,
        scratch=[pltpu.VMEM((1, tokens), jnp.int32), dma((3,))],
    )
    packed_low, bias, column = call(
        mask_kernel,
        [
            pltpu.VMEM((2 * cut, kv_width), bf16),
            pltpu.VMEM((tokens, tokens), f32),
            pltpu.VMEM((tokens, tokens), f32),
        ],
        [VMEM] * 3,
        (keys, values, doc_row),
        flops=2**27,
    )
    highs, lows = [], []
    for s in range(1, span):
        ring = [(i, (i + s) % place_count) for i in range(place_count)]
        highs.append(lax.ppermute(packed_high, "ctx", ring))
        lows.append(lax.ppermute(packed_low, "ctx", ring[: place_count - s]))

    other_core = [(i, i ^ 1) for i in range(devices)]

    def keep_shares(att, first, count, pieces, flops):
        keep = pltpu.VMEM((att.shape[0], block // pieces), bf16)
        return call(
            functools.partial(keep_kernel, first, count),
            [keep] * (count * pieces),
            [VMEM] * 2,
            (near(att), out_weight),
            flops=flops,
        )

    def add(keep, dtype, *got):
        return call(
            sum_kernel,
            pltpu.VMEM(keep.shape, dtype),
            [VMEM] * (1 + len(got)),
            tuple(map(near, (keep, *got))),
        )

    def outputs(rows, pieces):
        share = pltpu.VMEM((rows, block // pieces), bf16)
        return [pltpu.VMEM((rows, width), bf16)] + [share] * ((chips - 1) * pieces)

    always = (queries, keys, values, near(bias), near(column), out_weight)
    done = call(
        functools.partial(first_kernel, cut, chips, 1 + (chips - 1) * PIECES),
        outputs(tokens - cut, PIECES) + outputs(cut, 1),
        [VMEM] * len(always),
        always,
        flops=2**27,
    )

    def shares(rows, pieces, kernel, args, after):
        att, *gives = call(
            kernel,
            outputs(rows, pieces),
            [VMEM] * len(args) + [ANY] * len(after),
            (*args, *after),
            flops=8 * tokens * width * block,
        )
        keeps = keep_shares(att, 1, chips - 1, pieces, 2**33)
        sums, arrived = [], []
        for i, (keep, give) in enumerate(zip(keeps, gives)):
            total = add(keep, bf16, lax.ppermute(give, "head", other_core))
            step = (i // pieces + 1) * CORES
            sums.append(total)
            arrived.append(
                lax.ppermute(total, "head", [(j, (j + step) % devices) for j in range(devices)])
            )
        return att, sums, arrived

    n_done = 1 + (chips - 1) * PIECES
    att_high, sums, high = shares(
        tokens - cut,
        PIECES,
        functools.partial(give_kernel, cut, chips, n_done, len(highs), len(lows) - 1),
        (*always, *map(near, highs + lows[:-1] + list(done[:n_done]))),
        [],
    )
    state = pltpu.VMEM((groups, cut * (width // kv_width), HEAD_DIM), f32)
    states = call(
        own_kernel,
        [state] * 3,
        [VMEM] * 4,
        (queries, keys, values, near(bias)),
        flops=2**20,
    )
    att_low, sums, low = shares(
        cut,
        1,
        functools.partial(low_kernel, chips, chips, len(highs)),
        (
            *(queries, near(column), *map(near, states), out_weight),
            *map(near, highs + lows + list(done[n_done:])),
        ),
        sums,
    )

    att, *gives = call(
        local_kernel,
        [pltpu.VMEM((tokens, width), bf16)] + [pltpu.VMEM((tokens, block // 2), bf16)] * 2,
        [VMEM] * 3 + [ANY] * len(high),
        (near(att_low), near(att_high), out_weight, *high),
        flops=4 * tokens * width * block,
    )
    (keep,) = keep_shares(att, 0, 1, 1, 0)
    local = add(keep, f32, *[lax.ppermute(give, "head", other_core) for give in gives])

    def finish(first, rows, pieces, arrived, *out):
        return pl.pallas_call(
            functools.partial(final_kernel, first, pieces, len(arrived)),
            out_shape=pltpu.HBM((tokens, block), bf16),
            in_specs=[VMEM] * (1 + len(arrived)) + [HBM] * len(out),
            out_specs=HBM,
            scratch_shapes=[pltpu.VMEM((rows, block), bf16), dma],
            input_output_aliases={1 + len(arrived): 0} if out else {},
            cost_estimate=pl.CostEstimate(flops=0, bytes_accessed=0, transcendentals=0),
        )(near(local), *map(near, arrived), *out)

    return finish(0, cut, 1, low, finish(cut, tokens - cut, PIECES, high))


def solution(mesh):
    in_specs = (P("ctx", "head"), P("ctx", "head"), P("ctx", "head"), P("ctx"), P("head", None))
    out_specs = P("ctx", "head")
    return jax.shard_map(body, mesh=mesh, in_specs=in_specs, out_specs=out_specs, check_vma=False)
```

```python
import functools
import math

import jax
import jax.numpy as jnp
from jax import lax
from jax.experimental import pallas as pl
from jax.experimental.pallas import tpu as pltpu
from jax.sharding import PartitionSpec as P

HEAD_DIM = 128
CORES = 2
CUT = 176 / 256
DOC_ROWS = 16
PIECES = 1
LOG2_SCALE = math.log2(math.e) / math.sqrt(HEAD_DIM)
HIDDEN = -1e30
NT = (((1,), (1,)), ((), ()))
VMEM = pl.BlockSpec(memory_space=pltpu.VMEM)
ANY = pl.BlockSpec(memory_space=pl.ANY)
HBM = pl.BlockSpec(memory_space=pltpu.HBM)


def near(x):
    return pltpu.with_memory_space_constraint(x, pltpu.VMEM)


def far(x):
    return pltpu.with_memory_space_constraint(x, pltpu.HBM)


def call(kernel, out_shape, in_specs, args, flops=0, moved=0, vmem_mib=32, scratch=()):
    return pl.pallas_call(
        kernel,
        out_shape=out_shape,
        in_specs=in_specs,
        out_specs=jax.tree.map(lambda _: VMEM, out_shape),
        scratch_shapes=scratch,
        compiler_params=pltpu.CompilerParams(vmem_limit_bytes=vmem_mib * 2**20),
        cost_estimate=pl.CostEstimate(
            flops=flops, bytes_accessed=moved, transcendentals=0
        ),
    )(*args)


def pack_kernel(k_hbm, v_hbm, doc_hbm, high_ref, held, sem):
    tokens, width = k_hbm.shape
    rows = (high_ref.shape[0] - DOC_ROWS) // 2
    last = lax.axis_index("ctx") == lax.axis_size("ctx") - 1

    @pl.when(last)
    def _():
        high_ref[...] = jnp.zeros_like(high_ref)

    @pl.when(jnp.logical_not(last))
    def _():
        copies = [pltpu.make_async_copy(doc_hbm, held, sem.at[2])]
        for i, source in enumerate((k_hbm, v_hbm)):
            copies.append(
                pltpu.make_async_copy(
                    source.at[tokens - rows :], high_ref.at[i * rows : (i + 1) * rows], sem.at[i]
                )
            )
        for copy in copies:
            copy.start()
        copies[0].wait()
        docs = (held[...] + 1).astype(jnp.float32)
        parts = [docs[:, at : at + width] for at in range(0, tokens, width)]
        parts.append(jnp.zeros((DOC_ROWS - len(parts), width), jnp.float32))
        high_ref[2 * rows :, :] = jnp.concatenate(parts, axis=0).astype(jnp.bfloat16)
        for copy in copies[1:]:
            copy.wait()


def stacked(q_ref, r0, rows, first, repeats):
    heads = [
        q_ref[r0 : r0 + rows, h * HEAD_DIM : (h + 1) * HEAD_DIM]
        for h in range(first, first + repeats)
    ]
    return jnp.concatenate(heads, axis=0)


def with_ones(v):
    return jnp.concatenate([v, jnp.ones_like(v)], axis=1)


def hide(scores, bias):
    rows, count = bias.shape
    shape = (scores.shape[0] // rows, rows, count)
    return (scores.reshape(shape) + bias[None]).reshape(scores.shape)


def weights_of(scores, top):
    return jnp.exp2((scores - top) * LOG2_SCALE).astype(jnp.bfloat16)


def key_docs(high_ref, tokens):
    wide = high_ref[high_ref.shape[0] - DOC_ROWS :, :].astype(jnp.float32)
    parts = [wide[i : i + 1, :] for i in range(tokens // high_ref.shape[1])]
    return jnp.concatenate(parts, axis=1)


def attend(first, q_ref, bias_ref, column_ref, own_k, own_v, highs, lows, att_ref):
    tokens = q_ref.shape[0]
    rows = att_ref.shape[0]
    count = first + rows
    groups = own_k.shape[1] // HEAD_DIM
    repeats = q_ref.shape[1] // HEAD_DIM // groups
    column = column_ref[first:count, :]
    biases, keys, values = [], [], []
    for s, (high, low) in enumerate(zip(highs, lows), 1):
        n = (high.shape[0] - DOC_ROWS) // 2
        seen = tokens if low is not None else n
        if low is not None:
            keys.append(low[: tokens - n, :])
            values.append(low[tokens - n :, :])
        keys.append(high[:n, :])
        values.append(high[n : 2 * n, :])
        there = (lax.axis_index("ctx") >= s).astype(jnp.float32)
        same = key_docs(high, tokens)[:, tokens - seen :] * there == column[:, :seen]
        biases.append(jnp.where(same, 0.0, HIDDEN))
    place = 0 if first else len(biases)
    biases.insert(place, bias_ref[first:count, :count])
    keys.insert(place * 2, own_k[:count, :])
    values.insert(place * 2, own_v[:count, :])
    bias = jnp.concatenate(biases, axis=1)
    all_keys = jnp.concatenate(keys, axis=0)
    all_values = jnp.concatenate(values, axis=0)
    lanes = [slice(g * HEAD_DIM, (g + 1) * HEAD_DIM) for g in range(groups)]
    queries = [stacked(q_ref, first, rows, g * repeats, repeats) for g in range(groups)]
    scores = [
        lax.dot_general(q, all_keys[:, at], NT, preferred_element_type=jnp.float32)
        for q, at in zip(queries, lanes)
    ]
    scores = [hide(s, bias) for s in scores]
    tops = [jnp.max(s, axis=1, keepdims=True) for s in scores]
    weights = [weights_of(s, top) for s, top in zip(scores, tops)]
    summed = [
        jnp.dot(w, with_ones(all_values[:, at]), preferred_element_type=jnp.float32)
        for w, at in zip(weights, lanes)
    ]
    for g in range(groups):
        result = (summed[g][:, :HEAD_DIM] / summed[g][:, HEAD_DIM:]).astype(jnp.bfloat16)
        for r in range(repeats):
            h = g * repeats + r
            att_ref[:, h * HEAD_DIM : (h + 1) * HEAD_DIM] = result[r * rows : (r + 1) * rows]


def mask_kernel(k_ref, v_ref, doc_ref, low_ref, bias_ref, column_ref):
    tokens = doc_ref.shape[1]
    cut = low_ref.shape[0] // 2
    low_ref[:cut] = k_ref[:cut]
    low_ref[cut:] = v_ref[:cut]
    docs = jnp.broadcast_to(doc_ref[...].astype(jnp.float32) + 1.0, (tokens, tokens))
    columns = jnp.transpose(docs)
    at = lax.broadcasted_iota(jnp.int32, (tokens, tokens), 0)
    key = lax.broadcasted_iota(jnp.int32, (tokens, tokens), 1)
    bias_ref[...] = jnp.where((key <= at) & (docs == columns), 0.0, HIDDEN)
    column_ref[...] = columns


def own_kernel(q_ref, k_ref, v_ref, bias_ref, acc_ref, total_ref, top_ref):
    groups = k_ref.shape[1] // HEAD_DIM
    repeats = q_ref.shape[1] // HEAD_DIM // groups
    rows = acc_ref.shape[1] // repeats

    @pl.when(lax.axis_index("ctx") > 0)
    def _():
        lanes = [slice(g * HEAD_DIM, (g + 1) * HEAD_DIM) for g in range(groups)]
        scores = [
            lax.dot_general(
                stacked(q_ref, 0, rows, g * repeats, repeats),
                k_ref[:rows, lanes[g]],
                NT,
                preferred_element_type=jnp.float32,
            )
            for g in range(groups)
        ]
        scores = [hide(s, bias_ref[:rows, :rows]) for s in scores]
        tops = [jnp.max(s, axis=1, keepdims=True) for s in scores]
        weights = [weights_of(s, top) for s, top in zip(scores, tops)]
        for g in range(groups):
            summed = jnp.dot(
                weights[g], with_ones(v_ref[:rows, lanes[g]]), preferred_element_type=jnp.float32
            )
            acc_ref[g] = summed[:, :HEAD_DIM]
            total_ref[g] = summed[:, HEAD_DIM:]
            top_ref[g] = jnp.broadcast_to(tops[g], acc_ref.shape[1:])


def attend_before(q_ref, column_ref, state, highs, lows, att_ref):
    acc_ref, total_ref, top_ref = state
    tokens, width = q_ref.shape
    rows = att_ref.shape[0]
    groups = acc_ref.shape[0]
    repeats = width // HEAD_DIM // groups
    column = column_ref[:rows, :]
    biases, keys, values = [], [], []
    for s, (high, low) in enumerate(zip(highs, lows), 1):
        keys += [low[:rows, :], high[: tokens - rows, :]]
        values += [low[rows:, :], high[tokens - rows : 2 * (tokens - rows), :]]
        there = (lax.axis_index("ctx") >= s).astype(jnp.float32)
        same = key_docs(high, tokens) * there == column
        biases.append(jnp.where(same, 0.0, HIDDEN))
    bias = jnp.concatenate(biases, axis=1)
    all_keys = jnp.concatenate(keys, axis=0)
    all_values = jnp.concatenate(values, axis=0)
    spread = bias.shape[1] // HEAD_DIM
    lanes = [slice(g * HEAD_DIM, (g + 1) * HEAD_DIM) for g in range(groups)]
    scores = [
        lax.dot_general(
            stacked(q_ref, 0, rows, g * repeats, repeats),
            all_keys[:, lanes[g]],
            NT,
            preferred_element_type=jnp.float32,
        )
        for g in range(groups)
    ]
    scores = [hide(x, bias) for x in scores]
    tops = [
        jnp.maximum(top_ref[g], jnp.max(scores[g], axis=1, keepdims=True)) for g in range(groups)
    ]
    weights = [
        weights_of(x, jnp.concatenate([top] * spread, axis=1)) for x, top in zip(scores, tops)
    ]
    for g in range(groups):
        factor = jnp.exp2((top_ref[g] - tops[g]) * LOG2_SCALE)
        summed = jnp.dot(
            weights[g], with_ones(all_values[:, lanes[g]]), preferred_element_type=jnp.float32
        )
        acc = acc_ref[g] * factor + summed[:, :HEAD_DIM]
        total = total_ref[g] * factor + summed[:, HEAD_DIM:]
        result = (acc / total).astype(jnp.bfloat16)
        for r in range(repeats):
            h = g * repeats + r
            att_ref[:, h * HEAD_DIM : (h + 1) * HEAD_DIM] = result[r * rows : (r + 1) * rows]


def owner(d, which):
    chips = lax.axis_size("head") // CORES
    me = lax.axis_index("head")
    chip, core = me // CORES, me % CORES
    return lax.rem(chip + d, chips) * CORES + lax.rem(core + which, CORES)


def project(att, w_ref, d, which, out_refs):
    block = w_ref.shape[1] // lax.axis_size("head")
    start = pl.multiple_of(owner(d, which) * block, block)
    share = jnp.dot(att, w_ref[:, pl.ds(start, block)], preferred_element_type=jnp.float32)
    cols = block // len(out_refs)
    for i, ref in enumerate(out_refs):
        ref[...] = share[:, i * cols : (i + 1) * cols].astype(jnp.bfloat16)


def give_shares(first, chips, refs, highs, lows, w_ref, att_ref, gives):
    attend(first, *refs, highs, lows, att_ref)
    att = att_ref[...]
    pieces = len(gives) // (chips - 1)
    for d in range(1, chips):
        project(att, w_ref, d, 1, gives[(d - 1) * pieces : d * pieces])


def first_kernel(cut, chips, n_outs, q_ref, k_ref, v_ref, bias_ref, column_ref, w_ref, *outs):
    refs = (q_ref, bias_ref, column_ref, k_ref, v_ref)
    highs, lows = outs[:n_outs], outs[n_outs:]

    @pl.when(lax.axis_index("ctx") == 0)
    def _():
        for first, (att_ref, *gives) in ((cut, highs), (0, lows)):
            give_shares(first, chips, refs, [], [], w_ref, att_ref, gives)


def give_kernel(
    first, chips, n_outs, n_high, n_low, q_ref, k_ref, v_ref, bias_ref, column_ref, w_ref, *rest
):
    outs = rest[-n_outs:]
    highs, lows = list(rest[:n_high]), list(rest[n_high : n_high + n_low])
    done = rest[n_high + n_low : n_high + n_low + n_outs]
    lows += [None] * (n_high - n_low)
    refs = (q_ref, bias_ref, column_ref, k_ref, v_ref)
    here = lax.axis_index("ctx")

    @pl.when(here == 0)
    def _():
        for ref, out in zip(done, outs):
            out[...] = ref[...]

    @pl.when(here > 0)
    def _():
        give_shares(first, chips, refs, highs, lows, w_ref, outs[0], outs[1:])


def low_kernel(
    chips, n_outs, n_prev, q_ref, column_ref, acc_ref, total_ref, top_ref, w_ref, *rest
):
    outs = rest[-n_outs:]
    highs, lows = rest[:n_prev], rest[n_prev : 2 * n_prev]
    done = rest[2 * n_prev : 2 * n_prev + n_outs]
    here = lax.axis_index("ctx")

    @pl.when(here == 0)
    def _():
        for ref, out in zip(done, outs):
            out[...] = ref[...]

    @pl.when(here > 0)
    def _():
        att_ref, gives = outs[0], outs[1:]
        attend_before(q_ref, column_ref, (acc_ref, total_ref, top_ref), highs, lows, att_ref)
        att = att_ref[...]
        for d in range(1, chips):
            project(att, w_ref, d, 1, gives[d - 1 : d])


def keep_kernel(first, chips, att_ref, w_ref, *outs):
    att = att_ref[...]
    pieces = len(outs) // chips
    for i in range(chips):
        project(att, w_ref, first + i, 0, outs[i * pieces : (i + 1) * pieces])


def local_kernel(low_ref, high_ref, w_ref, *rest):
    att_ref, *gives = rest[-3:]
    rows = low_ref.shape[0]
    att_ref[:rows] = low_ref[...]
    att_ref[rows:] = high_ref[...]
    block = w_ref.shape[1] // lax.axis_size("head")
    cols = block // len(gives)
    for i, give_ref in enumerate(gives):
        start = pl.multiple_of(owner(0, 1) * block + i * cols, cols)
        give_ref[...] = jnp.dot(
            att_ref[...], w_ref[:, pl.ds(start, cols)], preferred_element_type=jnp.float32
        ).astype(jnp.bfloat16)


def sum_kernel(keep_ref, *rest):
    out_ref, at = rest[-1], 0
    for got in rest[:-1]:
        lanes = slice(at, at + got.shape[1])
        total = keep_ref[:, lanes].astype(jnp.float32) + got[...].astype(jnp.float32)
        out_ref[:, lanes] = total.astype(out_ref.dtype)
        at += got.shape[1]


def final_kernel(first, pieces, count, local_ref, *rest):
    out_hbm, held, sem = rest[-3:]
    rows, block = held.shape
    cols = block // pieces
    for i in range(pieces):
        here = slice(i * cols, (i + 1) * cols)
        total = local_ref[first : first + rows, here]
        for got in rest[i:count:pieces]:
            total = total + got[...].astype(jnp.float32)
        held[:, here] = total.astype(jnp.bfloat16)
    copy = pltpu.make_async_copy(held, out_hbm.at[pl.ds(first, rows)], sem)
    copy.start()
    copy.wait()


def body(queries, keys, values, segment_ids, out_weight):
    tokens, width = queries.shape
    kv_width = keys.shape[1]
    place_count = lax.axis_size("ctx")
    devices = lax.axis_size("head")
    chips = devices // CORES
    columns = out_weight.shape[1]
    block = columns // devices
    span = max(place_count // 16, 2)
    cut = int(tokens * CUT)
    bf16, f32 = jnp.bfloat16, jnp.float32
    dma = pltpu.SemaphoreType.DMA

    doc_row = segment_ids.reshape(1, tokens)
    groups = kv_width // HEAD_DIM
    packed_high = call(
        pack_kernel,
        pltpu.VMEM((2 * (tokens - cut) + DOC_ROWS, kv_width), bf16),
        [HBM] * 3,
        (far(keys), far(values), far(doc_row)),
        flops=2**33,
        scratch=[pltpu.VMEM((1, tokens), jnp.int32), dma((3,))],
    )
    packed_low, bias, column = call(
        mask_kernel,
        [
            pltpu.VMEM((2 * cut, kv_width), bf16),
            pltpu.VMEM((tokens, tokens), f32),
            pltpu.VMEM((tokens, tokens), f32),
        ],
        [VMEM] * 3,
        (keys, values, doc_row),
        flops=2**27,
    )
    highs, lows = [], []
    for s in range(1, span):
        ring = [(i, (i + s) % place_count) for i in range(place_count)]
        highs.append(lax.ppermute(packed_high, "ctx", ring))
        lows.append(lax.ppermute(packed_low, "ctx", ring[: place_count - s]))

    other_core = [(i, i ^ 1) for i in range(devices)]

    def keep_shares(att, first, count, pieces, flops):
        keep = pltpu.VMEM((att.shape[0], block // pieces), bf16)
        return call(
            functools.partial(keep_kernel, first, count),
            [keep] * (count * pieces),
            [VMEM] * 2,
            (near(att), out_weight),
            flops=flops,
        )

    def add(keep, dtype, *got):
        return call(
            sum_kernel,
            pltpu.VMEM(keep.shape, dtype),
            [VMEM] * (1 + len(got)),
            tuple(map(near, (keep, *got))),
        )

    def outputs(rows, pieces):
        share = pltpu.VMEM((rows, block // pieces), bf16)
        return [pltpu.VMEM((rows, width), bf16)] + [share] * ((chips - 1) * pieces)

    always = (queries, keys, values, near(bias), near(column), out_weight)
    done = call(
        functools.partial(first_kernel, cut, chips, 1 + (chips - 1) * PIECES),
        outputs(tokens - cut, PIECES) + outputs(cut, 1),
        [VMEM] * len(always),
        always,
        flops=2**27,
    )

    def shares(rows, pieces, kernel, args, after):
        att, *gives = call(
            kernel,
            outputs(rows, pieces),
            [VMEM] * len(args) + [ANY] * len(after),
            (*args, *after),
            flops=8 * tokens * width * block,
        )
        keeps = keep_shares(att, 1, chips - 1, pieces, 2**33)
        sums, arrived = [], []
        for i, (keep, give) in enumerate(zip(keeps, gives)):
            total = add(keep, bf16, lax.ppermute(give, "head", other_core))
            step = (i // pieces + 1) * CORES
            sums.append(total)
            arrived.append(
                lax.ppermute(total, "head", [(j, (j + step) % devices) for j in range(devices)])
            )
        return att, sums, arrived

    n_done = 1 + (chips - 1) * PIECES
    att_high, sums, high = shares(
        tokens - cut,
        PIECES,
        functools.partial(give_kernel, cut, chips, n_done, len(highs), len(lows) - 1),
        (*always, *map(near, highs + lows[:-1] + list(done[:n_done]))),
        [],
    )
    state = pltpu.VMEM((groups, cut * (width // kv_width), HEAD_DIM), f32)
    states = call(
        own_kernel,
        [state] * 3,
        [VMEM] * 4,
        (queries, keys, values, near(bias)),
        flops=2**20,
    )
    att_low, sums, low = shares(
        cut,
        1,
        functools.partial(low_kernel, chips, chips, len(highs)),
        (
            *(queries, near(column), *map(near, states), out_weight),
            *map(near, highs + lows + list(done[n_done:])),
        ),
        sums,
    )

    att, *gives = call(
        local_kernel,
        [pltpu.VMEM((tokens, width), bf16)] + [pltpu.VMEM((tokens, block // 2), bf16)] * 2,
        [VMEM] * 3 + [ANY] * len(high),
        (near(att_low), near(att_high), out_weight, *high),
        flops=4 * tokens * width * block,
    )
    (keep,) = keep_shares(att, 0, 1, 1, 0)
    local = add(keep, f32, *[lax.ppermute(give, "head", other_core) for give in gives])

    def finish(first, rows, pieces, arrived, *out):
        return pl.pallas_call(
            functools.partial(final_kernel, first, pieces, len(arrived)),
            out_shape=pltpu.HBM((tokens, block), bf16),
            in_specs=[VMEM] * (1 + len(arrived)) + [HBM] * len(out),
            out_specs=HBM,
            scratch_shapes=[pltpu.VMEM((rows, block), bf16), dma],
            input_output_aliases={1 + len(arrived): 0} if out else {},
            cost_estimate=pl.CostEstimate(flops=0, bytes_accessed=0, transcendentals=0),
        )(near(local), *map(near, arrived), *out)

    return finish(0, cut, 1, low, finish(cut, tokens - cut, PIECES, high))


def solution(mesh):
    in_specs = (P("ctx", "head"), P("ctx", "head"), P("ctx", "head"), P("ctx"), P("head", None))
    out_specs = P("ctx", "head")
    return jax.shard_map(body, mesh=mesh, in_specs=in_specs, out_specs=out_specs, check_vma=False)
```
